128 devices in a mesh: section: 2 (over core), dp: 8 (over z, x_lo), tensor: 8 (over y, x_hi).
Axes of the slice: x: 4 (x_hi: 2, x_lo: 2; x = x_hi * 2 + x_lo), y: 4, z: 4, core: 2. Of those that a mesh axis runs over, the one named last changes fastest.
Arguments:
- upstream: bfloat16 [2, 512, 8192], P('section', ('dp', 'tensor')), may hold values from -1.5 to 1.5
- saved_input: bfloat16 [2, 512, 8192], P('section', ('dp', 'tensor')), may hold values from -400 to 400
- norm_gain: bfloat16 [2, 8192], P('section'), may hold values from 0.099609375 to 1.8984375
- up_weight: bfloat16 [2, 8192, 16384], P('section', None, ('dp', 'tensor')), may hold values from -0.0625 to 0.0625
- down_weight: bfloat16 [2, 16384, 8192], P('section', ('dp', 'tensor')), may hold values from -0.046875 to 0.046875
Outputs:
- input_grad: bfloat16 [2, 512, 8192], P('section', ('dp', 'tensor'))
- up_grad: float32 [2, 8192, 16384], P('section', None, ('dp', 'tensor'))
- down_grad: float32 [2, 16384, 8192], P('section', ('dp', 'tensor'))
- gain_grad: float32 [2, 8192], P('section')
The draws below stay inside these ranges and needn't reach their ends.
All inputs are finite; a program needn't handle non-finite values.
Results may differ from the reference program's by a relative error of at most 0.015.
Values may be sent and summed in bfloat16 or wider, within the bound.
A program may use at most 128 MiB of HBM per device.

```python
import jax
import jax.numpy as jnp
from jax import lax

D = 8192
FF = 16384
TOKENS = 512
N_DP = 8


def draw_saved_input(key, part):
    key = jax.random.fold_in(key, 11)
    base_key, column_key, row_key = jax.random.split(key, 3)
    column_scale = jnp.exp(jax.random.uniform(column_key, (2, 1, D), jnp.float32, 0.0, 2.3))
    row_scale = jnp.exp(jax.random.uniform(row_key, (2, TOKENS, 1), jnp.float32, 0.0, 2.3))
    base_values = jnp.clip(jax.random.normal(base_key, (2, TOKENS, D), jnp.float32), -4.0, 4.0)
    return (base_values * column_scale * row_scale).astype(jnp.bfloat16)


def level_of(key, dims, cuts, least, top_value):
    level = 1.0
    for dim, blocks in cuts:
        draws = jax.random.uniform(jax.random.fold_in(jax.random.fold_in(key, 6), dim), (blocks,), jnp.float32, least / len(cuts), top_value / len(cuts))
        level = level * jnp.repeat(jnp.exp(draws), dims[dim] // blocks).reshape((-1,) + (1,) * (len(dims) - 1 - dim))
    return level


def noise(own_key, extent, deviation, most, shards=(), kind=jnp.bfloat16):
    entries = deviation * jax.random.normal(own_key, extent, jnp.float32)
    if shards:
        entries = entries * level_of(own_key, extent, shards, -0.22, 0.18)
    return jnp.clip(entries, -most, most).astype(kind)


def setup_inputs(seed: int = 0) -> dict:
    streams_of = jax.random.split(jax.random.key(seed), 6)
    return {
        "upstream": noise(streams_of[0], (2, TOKENS, D), 0.25, 1.5, ((0, 2), (1, 64))),
        "saved_input": draw_saved_input(jax.random.fold_in(streams_of[5], 71), 0),
        "norm_gain": jnp.clip(1.0 + 0.18 * jax.random.normal(streams_of[2], (2, D), jnp.float32), 0.099609375, 1.8984375).astype(jnp.bfloat16),
        "up_weight": noise(streams_of[3], (2, D, FF), D ** -0.5, 0.0625, ((0, 2), (2, 64))),
        "down_weight": noise(streams_of[4], (2, FF, D), FF ** -0.5, 0.046875, ((0, 2), (1, 64))),
    }


gelu_scale = 0.7978845608028654
cubic_coef = 0.044715

def gelu_pair(hidden):
    tanh_part = jnp.tanh(gelu_scale * (hidden + cubic_coef * hidden * hidden * hidden))
    gelu_out = 0.5 * hidden * (1.0 + tanh_part)
    derivative = 0.5 * (1.0 + tanh_part) + 0.5 * hidden * (1.0 - tanh_part * tanh_part) * gelu_scale * (1.0 + 3.0 * cubic_coef * hidden * hidden)
    return (gelu_out, derivative)

def normalize(row_values):
    row_mean = lax.optimization_barrier(jnp.mean(row_values, axis=-1, keepdims=True))
    centered = row_values - row_mean
    variance = lax.optimization_barrier(jnp.mean(centered * centered, axis=-1, keepdims=True))
    inverse = lax.rsqrt(variance + 1e-05)
    return (centered * inverse, inverse)

def reorder(tokens_full, grid_side):
    tok_count = tokens_full.shape[0]
    feat_width = tokens_full.shape[1]
    token_blocks = tokens_full.reshape(grid_side, grid_side, tok_count // (grid_side * grid_side), feat_width)
    return jnp.swapaxes(token_blocks, 0, 1).reshape(tok_count, feat_width)

def section_backward(grad_in, saved_rows, gain_row, up_matrix, down_matrix):
    unit_rows, inverse = normalize(saved_rows.astype(jnp.float32))
    gain_wide = gain_row.astype(jnp.float32)
    normed = (unit_rows * gain_wide).astype(jnp.bfloat16)
    hidden = jnp.dot(normed, up_matrix, preferred_element_type=jnp.float32)
    act_value, derivative = gelu_pair(hidden)
    activation = act_value.astype(jnp.bfloat16)
    grad_act = jnp.dot(grad_in, down_matrix.T, preferred_element_type=jnp.float32)
    grad_hidden = (grad_act * derivative).astype(jnp.bfloat16)
    down_grad = jnp.dot(activation.T, grad_in, preferred_element_type=jnp.float32)
    up_grad = jnp.dot(normed.T, grad_hidden, preferred_element_type=jnp.float32)
    grad_normed = jnp.dot(grad_hidden, up_matrix.T, preferred_element_type=jnp.float32)
    gain_grad = lax.optimization_barrier(jnp.sum(grad_normed * unit_rows, axis=0))
    grad_scaled = grad_normed * gain_wide
    inner_mean = lax.optimization_barrier(jnp.mean(grad_scaled, axis=-1, keepdims=True))
    proj_mean = lax.optimization_barrier(jnp.mean(grad_scaled * unit_rows, axis=-1, keepdims=True))
    grad_input = inverse * (grad_scaled - inner_mean - unit_rows * proj_mean)
    input_grad = (grad_in.astype(jnp.float32) + grad_input).astype(jnp.bfloat16)
    return (input_grad, up_grad, down_grad, gain_grad)

def reference(upstream, saved_input, norm_gain, up_weight, down_weight):
    outputs = [section_backward(reorder(upstream[1 - section_idx], N_DP), saved_input[section_idx], norm_gain[section_idx], up_weight[section_idx], down_weight[section_idx]) for section_idx in range(2)]
    return (jnp.stack([outputs[0][0], outputs[1][0]]), jnp.stack([outputs[0][1], outputs[1][1]]), jnp.stack([outputs[0][2], outputs[1][2]]), jnp.stack([outputs[0][3], outputs[1][3]]))
```

```python
import jax
import jax.numpy as jnp
from jax import lax
from jax.experimental import pallas as pl
from jax.experimental.pallas import tpu as pltpu
from jax.sharding import PartitionSpec as P

gelu_scale = 0.7978845608028654
cubic_coef = 0.044715

D = 8192
HALF = D // 2
HID = 256
ROWS = 8
MESH = pl.DeviceIdType.MESH

ORDERS = ((2, 1, 0), (0, 2, 1), (1, 0, 2))


def cut(tiles):
    subs, at = [], 0
    for number, count in enumerate(tiles):
        subs.append((ORDERS[number // 2], 1 if number % 2 == 0 else -1, at * 128, count * 128))
        at += count
    return tuple(subs)


GATHER = cut((11, 11, 11, 10, 11, 10))
SCATTER = cut((6, 5, 6, 5, 5, 5))
SUBS = range(6)


def gelu_pair(hidden):
    tanh_part = jnp.tanh(gelu_scale * (hidden + cubic_coef * hidden * hidden * hidden))
    gelu_out = 0.5 * hidden * (1.0 + tanh_part)
    derivative = 0.5 * (1.0 + tanh_part) + 0.5 * hidden * (
        1.0 - tanh_part * tanh_part
    ) * gelu_scale * (1.0 + 3.0 * cubic_coef * hidden * hidden)
    return (gelu_out, derivative)


def f32(value):
    return value.astype(jnp.float32)


def kernel(
    upstream, saved, gain, up_hbm, down_hbm,
    input_grad, gain_grad, up_grad, down_grad,
    tokens, up, down, part, got0, got1, got2, hid, weights, sent_rows, arrived_rows, unit, total, gain_acc, gain_slots,
    up_stage, down_stage,
    load_sem, swap_sem, stage_sem, ag_send, ag_recv, rs_send, rs_recv, gain_send, gain_recv,
):
    section = lax.axis_index("section")
    dp = lax.axis_index("dp")
    tensor = lax.axis_index("tensor")
    place = (dp // 2, tensor // 2, (tensor % 2) * 2 + dp % 2)

    def device_at(z, y, x):
        return (section, z * 2 + x % 2, y * 2 + x // 2)

    def moved(axis, by):
        return lax.rem(place[axis] + (by + 4), 4)

    def neighbour(axis, by):
        there = list(place)
        there[axis] = moved(axis, by)
        return device_at(*there)

    partner = (1 - section, dp, tensor)

    barrier = pltpu.get_barrier_semaphore()
    others = [neighbour(axis, by) for axis in range(3) for by in (1, 2, 3)] + [partner]
    for other in others:
        pl.semaphore_signal(barrier, inc=1, device_id=other, device_id_type=MESH)
    load_up = pltpu.make_async_copy(up_hbm, up, load_sem.at[0])
    load_down = pltpu.make_async_copy(down_hbm, down, load_sem.at[1])
    load_up.start()
    load_down.start()
    sent_rows[...] = f32(upstream[...])
    pl.semaphore_wait(barrier, len(others))

    swap = pltpu.make_async_remote_copy(
        src_ref=sent_rows, dst_ref=arrived_rows, send_sem=swap_sem.at[0], recv_sem=swap_sem.at[1],
        device_id=partner, device_id_type=MESH,
    )
    swap.start()

    rows = f32(saved[...])
    centered = rows - jnp.mean(rows, axis=-1, keepdims=True)
    inverse = lax.rsqrt(jnp.mean(centered * centered, axis=-1, keepdims=True) + 1e-05)
    unit[...] = centered * inverse
    normed = unit[...] * f32(gain[...])
    swap.wait_recv()
    tokens[place[0], place[1], place[2]] = jnp.concatenate([normed, arrived_rows[...]], axis=0).astype(jnp.bfloat16)

    hid[...] = jnp.zeros_like(hid)

    def gathered(phase, sub, where):
        order, _, lo, size = GATHER[sub]
        index = [slice(None)] * 3
        for later in range(phase, 3):
            index[order[later]] = place[order[later]]
        index[order[phase]] = where
        return tokens.at[(*index, slice(None), pl.ds(lo, size))]

    def ag_copy(phase, sub, message, where, by):
        block = gathered(phase, sub, where)
        return pltpu.make_async_remote_copy(
            src_ref=block, dst_ref=block,
            send_sem=ag_send.at[phase, sub, message], recv_sem=ag_recv.at[phase, sub, message],
            device_id=neighbour(GATHER[sub][0][phase], by), device_id_type=MESH,
        )

    def ag_start(phase, sub):
        axis, way = GATHER[sub][0][phase], GATHER[sub][1]
        ag_copy(phase, sub, 0, place[axis], way).start()
        ag_copy(phase, sub, 1, place[axis], -way).start()

    def ag_forward(phase, sub):
        axis, way = GATHER[sub][0][phase], GATHER[sub][1]
        copy = ag_copy(phase, sub, 0, moved(axis, -way), way)
        copy.wait_recv()
        ag_copy(phase, sub, 2, moved(axis, -way), way).start()

    def ag_wait(phase, sub, message):
        axis, way = GATHER[sub][0][phase], GATHER[sub][1]
        ag_copy(phase, sub, message, moved(axis, way if message == 1 else 2), way).wait_recv()

    def plane(order, where):
        index = [slice(None)] * 3
        index[order[2]] = where
        return tuple(index)

    def first_products(sub, where):
        order, _, lo, size = GATHER[sub]
        at = plane(order, where)
        block = tokens[(*at, slice(None), pl.ds(lo, size))].reshape(256, size)
        above = jnp.dot(block, up[pl.ds(lo, size), :], preferred_element_type=jnp.float32)
        hid[(*at, pl.ds(0, 8), pl.ds(0, HID))] += above.reshape(4, 4, 16, HID)[:, :, :8]
        below = lax.dot_general(
            block, down[:, pl.ds(lo, size)], (((1,), (1,)), ((), ())), preferred_element_type=jnp.float32
        )
        hid[(*at, pl.ds(8, 8), pl.ds(HID, HID))] += below.reshape(4, 4, 16, HID)[:, :, 8:]

    for sub in SUBS:
        ag_start(0, sub)
    for phase in (0, 1):
        for sub in SUBS:
            ag_forward(phase, sub)
        for sub in SUBS:
            ag_wait(phase, sub, 1)
            ag_wait(phase, sub, 2)
            ag_start(phase + 1, sub)
    load_up.wait()
    load_down.wait()
    for sub in SUBS:
        first_products(sub, moved(GATHER[sub][0][2], 0))
    for sub in SUBS:
        ag_forward(2, sub)
    for sub in SUBS:
        first_products(sub, moved(GATHER[sub][0][2], -GATHER[sub][1]))
    for sub in SUBS:
        ag_wait(2, sub, 1)
        first_products(sub, moved(GATHER[sub][0][2], GATHER[sub][1]))
    for sub in SUBS:
        ag_wait(2, sub, 2)
        first_products(sub, moved(GATHER[sub][0][2], 2))

    SWAPPED = (0, 2, 1, 3)

    def activate(step, carry):
        z, y = step // 4, step % 4
        act, derivative = gelu_pair(hid[z, y, :, 0:8, 0:HID])
        for x in range(4):
            hid[z, y, x, 0:8, HID:] = hid[y, z, SWAPPED[x], 8:16, HID:] * derivative[x]
            hid[z, y, x, 0:8, 0:HID] = act[x]
        return carry

    lax.fori_loop(0, 16, activate, 0)

    def lay_out(step, carry):
        z, y = step // 4, step % 4
        blank = jnp.zeros((8, HID), jnp.float32)
        for x in range(4):
            weights[z, y, x, :, 0:HID] = jnp.concatenate([hid[z, y, x, 0:8, HID:], blank], axis=0).astype(jnp.bfloat16)
            weights[z, y, x, :, HID:] = jnp.concatenate(
                [blank, hid[y, z, SWAPPED[x], 0:8, 0:HID]], axis=0
            ).astype(jnp.bfloat16)
        return carry

    def second_products(sub, where):
        order, _, lo, size = SCATTER[sub]
        at = plane(order, where)
        left = hid[(*at, pl.ds(0, 8), pl.ds(HID, HID))].reshape(128, HID).astype(jnp.bfloat16)
        halves = []
        for start in (lo, HALF + lo):
            halves.append(
                lax.dot_general(
                    left, up[pl.ds(start, size), :], (((1,), (1,)), ((), ())), preferred_element_type=jnp.float32
                ).reshape(4, 4, 8, size)
            )
        part[(*at, slice(None), pl.ds(lo, size))] = jnp.concatenate(halves, axis=2).astype(jnp.bfloat16)

    GOT = (got0, got1, got2)

    def landing(phase, sub, message):
        _, _, lo, size = SCATTER[sub]
        ref = GOT[phase]
        return ref.at[(message, *([slice(None)] * (2 - phase)), slice(None), pl.ds(lo, size))]

    def share(phase, sub, where):
        order, _, lo, size = SCATTER[sub]
        columns = (slice(None), pl.ds(lo, size))
        if phase == 0:
            return part.at[(*plane(order, where), *columns)]
        if phase == 1:
            index = tuple(where if axis == order[1] else slice(None) for axis in range(3) if axis != order[2])
            return got0.at[(2, *index, *columns)]
        return got1.at[(2, where, *columns)]

    def rs_copy(phase, sub, message):
        order, way = SCATTER[sub][0], SCATTER[sub][1]
        axis = order[2 - phase]
        if message == 0:
            source, by = share(phase, sub, moved(axis, 2)), -way
        elif message == 1:
            source, by = share(phase, sub, moved(axis, way)), way
        else:
            source, by = landing(phase, sub, 0), -way
        return pltpu.make_async_remote_copy(
            src_ref=source, dst_ref=landing(phase, sub, message),
            send_sem=rs_send.at[phase, sub, message], recv_sem=rs_recv.at[phase, sub, message],
            device_id=neighbour(axis, by), device_id_type=MESH,
        )

    def rs_forward(phase, sub):
        order, way = SCATTER[sub][0], SCATTER[sub][1]
        rs_copy(phase, sub, 0).wait_recv()
        ref = landing(phase, sub, 0)
        mine = share(phase, sub, moved(order[2 - phase], -way))
        ref[...] = (f32(ref[...]) + f32(mine[...])).astype(jnp.bfloat16)
        rs_copy(phase, sub, 2).start()

    def rs_sum(phase, sub):
        order = SCATTER[sub][0]
        rs_copy(phase, sub, 1).wait_recv()
        rs_copy(phase, sub, 2).wait_recv()
        mine = share(phase, sub, moved(order[2 - phase], 0))
        return f32(mine[...]) + f32(landing(phase, sub, 1)[...]) + f32(landing(phase, sub, 2)[...])

    for sub in SUBS:
        second_products(sub, moved(SCATTER[sub][0][2], 2))
        rs_copy(0, sub, 0).start()
    for sub in SUBS:
        second_products(sub, moved(SCATTER[sub][0][2], SCATTER[sub][1]))
        rs_copy(0, sub, 1).start()
    for sub in SUBS:
        second_products(sub, moved(SCATTER[sub][0][2], -SCATTER[sub][1]))
    lax.fori_loop(0, 16, lay_out, 0)

    TILE = 512

    def stage_copies(step):
        slot = lax.rem(step, 2)
        at = pl.ds(pl.multiple_of(step * TILE, TILE), TILE)
        return (
            pltpu.make_async_copy(up_stage.at[slot], up_grad.at[at, :], stage_sem.at[0, slot]),
            pltpu.make_async_copy(down_stage.at[slot], down_grad.at[:, at], stage_sem.at[1, slot]),
        )

    def weight_tile(step, carry):
        slot = lax.rem(step, 2)

        @pl.when(step >= 2)
        def _():
            for copy in stage_copies(step - 2):
                copy.wait()

        block = tokens[:, :, :, :, pl.ds(pl.multiple_of(step * TILE, TILE), TILE)].reshape(1024, TILE)
        up_stage[slot] = lax.dot_general(
            block, weights[:, :, :, :, 0:HID].reshape(1024, HID), (((0,), (0,)), ((), ())),
            preferred_element_type=jnp.float32,
        )
        down_stage[slot] = lax.dot_general(
            weights[:, :, :, :, HID:].reshape(1024, HID), block, (((0,), (0,)), ((), ())),
            preferred_element_type=jnp.float32,
        )
        for copy in stage_copies(step):
            copy.start()
        return carry

    lax.fori_loop(0, 4, weight_tile, 0)
    for sub in SUBS:
        rs_forward(0, sub)
    for sub in SUBS:
        second_products(sub, moved(SCATTER[sub][0][2], 0))

    def gain_tile(step, carry):
        at = pl.ds(pl.multiple_of(step * 256, 256), 256)
        also = pl.ds(pl.multiple_of(HALF + step * 256, 256), 256)
        sums = [jnp.zeros((8, 256), jnp.float32)] * 2
        for z in range(4):
            here = f32(part[z, :, :, :, at]).reshape(16, 16, 256)
            for half, columns in enumerate((at, also)):
                rows = f32(tokens[z, :, :, :, columns]).reshape(16, 16, 256)[:, :8]
                sums[half] = sums[half] + jnp.sum(here[:, 8 * half : 8 * half + 8] * rows, axis=0)
        gain_acc[:, at] = sums[0]
        gain_acc[:, also] = sums[1]
        return carry

    lax.fori_loop(0, HALF // 256, gain_tile, 0)
    gain_slots[0, place[2]] = jnp.sum(gain_acc[...], axis=0, keepdims=True) / f32(gain[...])

    def gain_copy(phase, by, owner):
        axis = 2 - phase
        return pltpu.make_async_remote_copy(
            src_ref=gain_slots.at[phase, owner], dst_ref=gain_slots.at[phase, owner],
            send_sem=gain_send.at[phase, by - 1], recv_sem=gain_recv.at[phase, by - 1],
            device_id=neighbour(axis, by), device_id_type=MESH,
        )

    def gain_start(phase):
        for by in (1, 2, 3):
            gain_copy(phase, by, place[2 - phase]).start()

    def gain_sum(phase):
        for by in (1, 2, 3):
            gain_copy(phase, by, moved(2 - phase, -by)).wait_recv()
        return (gain_slots[phase, 0] + gain_slots[phase, 1]) + (gain_slots[phase, 2] + gain_slots[phase, 3])

    gain_start(0)
    lax.fori_loop(4, 8, weight_tile, 0)
    gain_slots[1, place[1]] = gain_sum(0)
    gain_start(1)
    lax.fori_loop(8, 12, weight_tile, 0)
    gain_slots[2, place[0]] = gain_sum(1)
    gain_start(2)
    lax.fori_loop(12, 16, weight_tile, 0)
    gain_grad[...] = gain_sum(2)

    for phase in (0, 1):
        for sub in SUBS:
            landing(phase, sub, 2)[...] = rs_sum(phase, sub).astype(jnp.bfloat16)
            rs_copy(phase + 1, sub, 0).start()
            rs_copy(phase + 1, sub, 1).start()
        for sub in SUBS:
            rs_forward(phase + 1, sub)
    for sub in SUBS:
        _, _, lo, size = SCATTER[sub]
        summed = rs_sum(2, sub)
        total[:, pl.ds(lo, size)] = summed[:8]
        total[:, pl.ds(HALF + lo, size)] = summed[8:]

    scaled = total[...] * f32(gain[...])
    units = unit[...]
    inner_mean = jnp.mean(scaled, axis=-1, keepdims=True)
    proj_mean = jnp.mean(scaled * units, axis=-1, keepdims=True)
    change = inverse * (scaled - inner_mean - units * proj_mean)
    own = f32(tokens[place[1], place[0], (place[2] % 2) * 2 + place[2] // 2])[8:]
    input_grad[...] = (own + change).astype(jnp.bfloat16)

    for step in (14, 15):
        for copy in stage_copies(step):
            copy.wait()
    swap.wait_send()
    for phase in range(3):
        for sub in SUBS:
            axis, way = GATHER[sub][0][phase], GATHER[sub][1]
            ag_copy(phase, sub, 0, place[axis], way).wait_send()
            ag_copy(phase, sub, 1, place[axis], -way).wait_send()
            ag_copy(phase, sub, 2, moved(axis, -way), way).wait_send()
            for message in range(3):
                rs_copy(phase, sub, message).wait_send()
        for by in (1, 2, 3):
            gain_copy(phase, by, place[2 - phase]).wait_send()


def on_device(upstream, saved_input, norm_gain, up_weight, down_weight):
    bf16, f4 = jnp.bfloat16, jnp.float32
    vmem, hbm = pl.BlockSpec(memory_space=pltpu.VMEM), pl.BlockSpec(memory_space=pl.ANY)
    dma = pltpu.SemaphoreType.DMA
    input_grad, gain_grad, up_grad, down_grad = pl.pallas_call(
        kernel,
        out_shape=[
            jax.ShapeDtypeStruct((ROWS, D), bf16),
            jax.ShapeDtypeStruct((1, D), f4),
            jax.ShapeDtypeStruct((D, HID), f4),
            jax.ShapeDtypeStruct((HID, D), f4),
        ],
        in_specs=[vmem, vmem, vmem, hbm, hbm],
        out_specs=[vmem, vmem, hbm, hbm],
        scratch_shapes=[
            pltpu.VMEM((4, 4, 4, 16, D), bf16),
            pltpu.VMEM((D, HID), bf16),
            pltpu.VMEM((HID, D), bf16),
            pltpu.VMEM((4, 4, 4, 16, HALF), bf16),
            pltpu.VMEM((3, 4, 4, 16, HALF), bf16),
            pltpu.VMEM((3, 4, 16, HALF), bf16),
            pltpu.VMEM((3, 16, HALF), bf16),
            pltpu.VMEM((4, 4, 4, 16, 2 * HID), f4),
            pltpu.VMEM((4, 4, 4, 16, 2 * HID), bf16),
            pltpu.VMEM((ROWS, D), f4),
            pltpu.VMEM((ROWS, D), f4),
            pltpu.VMEM((ROWS, D), f4),
            pltpu.VMEM((ROWS, D), f4),
            pltpu.VMEM((ROWS, D), f4),
            pltpu.VMEM((3, 4, 1, D), f4),
            pltpu.VMEM((2, 512, HID), f4),
            pltpu.VMEM((2, HID, 512), f4),
            dma((2,)), dma((2,)), dma((2, 2)),
            dma((3, 6, 3)), dma((3, 6, 3)), dma((3, 6, 3)), dma((3, 6, 3)),
            dma((3, 3)), dma((3, 3)),
        ],
        compiler_params=pltpu.CompilerParams(
            collective_id=0, has_side_effects=True, vmem_limit_bytes=60 * 2**20
        ),
        name="section_backward",
    )(upstream[0], saved_input[0], norm_gain, up_weight[0], down_weight[0])
    return (input_grad[None], up_grad[None], down_grad[None], gain_grad)


def solution(mesh):
    in_specs = (
        P("section", ("dp", "tensor"), None),
        P("section", ("dp", "tensor"), None),
        P("section", None),
        P("section", None, ("dp", "tensor")),
        P("section", ("dp", "tensor"), None),
    )
    out_specs = (
        P("section", ("dp", "tensor"), None),
        P("section", None, ("dp", "tensor")),
        P("section", ("dp", "tensor"), None),
        P("section", None),
    )
    return jax.shard_map(
        on_device, mesh=mesh, in_specs=in_specs, out_specs=out_specs, check_vma=False
    )
```

```python
import jax
import jax.numpy as jnp
from jax import lax
from jax.experimental import pallas as pl
from jax.experimental.pallas import tpu as pltpu
from jax.sharding import PartitionSpec as P

gelu_scale = 0.7978845608028654
cubic_coef = 0.044715

D = 8192
HALF = D // 2
HID = 256
ROWS = 8
MESH = pl.DeviceIdType.MESH

ORDERS = ((2, 1, 0), (0, 2, 1), (1, 0, 2))


def cut(tiles):
    subs, at = [], 0
    for number, count in enumerate(tiles):
        subs.append((ORDERS[number // 2], 1 if number % 2 == 0 else -1, at * 128, count * 128))
        at += count
    return tuple(subs)


GATHER = cut((11, 11, 10, 11, 11, 10))
SCATTER = cut((6, 5, 6, 5, 5, 5))
SUBS = range(6)


def gelu_pair(hidden):
    tanh_part = jnp.tanh(gelu_scale * (hidden + cubic_coef * hidden * hidden * hidden))
    gelu_out = 0.5 * hidden * (1.0 + tanh_part)
    derivative = 0.5 * (1.0 + tanh_part) + 0.5 * hidden * (
        1.0 - tanh_part * tanh_part
    ) * gelu_scale * (1.0 + 3.0 * cubic_coef * hidden * hidden)
    return (gelu_out, derivative)


def f32(value):
    return value.astype(jnp.float32)


def kernel(
    upstream, saved, gain, up_hbm, down_hbm,
    up_grad, down_grad, total, unit, inverse, own, gain_grad,
    tokens, weights, up, part, got0, got1, got2, hid, sent_rows, arrived_rows, gain_acc, gain_slots,
    load_sem, swap_sem, ag_send, ag_recv, rs_send, rs_recv, gain_send, gain_recv,
):
    section = lax.axis_index("section")
    dp = lax.axis_index("dp")
    tensor = lax.axis_index("tensor")
    place = (dp // 2, tensor // 2, (tensor % 2) * 2 + dp % 2)
    started = []

    def go(copy):
        copy.start()
        started.append(copy)

    def device_at(z, y, x):
        return (section, z * 2 + x % 2, y * 2 + x // 2)

    def moved(axis, by):
        return lax.rem(place[axis] + (by + 4), 4)

    def neighbour(axis, by):
        there = list(place)
        there[axis] = moved(axis, by)
        return device_at(*there)

    partner = (1 - section, dp, tensor)

    barrier = pltpu.get_barrier_semaphore()
    others = [neighbour(axis, by) for axis in range(3) for by in (1, 2, 3)] + [partner]
    for other in others:
        pl.semaphore_signal(barrier, inc=1, device_id=other, device_id_type=MESH)
    sent_rows[...] = f32(upstream[...])
    rows = f32(saved[...])
    centered = rows - jnp.mean(rows, axis=-1, keepdims=True)
    spread = lax.rsqrt(jnp.mean(centered * centered, axis=-1, keepdims=True) + 1e-05)
    inverse[...] = jnp.broadcast_to(spread, inverse.shape)
    unit[...] = centered * spread
    pl.semaphore_wait(barrier, len(others))

    swap = pltpu.make_async_remote_copy(
        src_ref=sent_rows, dst_ref=arrived_rows, send_sem=swap_sem.at[0], recv_sem=swap_sem.at[1],
        device_id=partner, device_id_type=MESH,
    )
    go(swap)
    normed = unit[...] * f32(gain[...])
    swap.wait_recv()
    tokens[place[0], place[1], place[2]] = jnp.concatenate([normed, arrived_rows[...]], axis=0).astype(jnp.bfloat16)

    def gathered(phase, sub, unit_by, where):
        order, _, lo, size = GATHER[sub]
        index = [slice(None)] * 3
        for later in range(phase, 3):
            index[order[later]] = place[order[later]]
        if phase:
            index[order[phase - 1]] = moved(order[phase - 1], unit_by)
        index[order[phase]] = where
        return tokens.at[(*index, slice(None), pl.ds(lo, size))]

    def slot(phase, unit_by):
        return 0 if phase == 0 else 4 * phase - 3 + unit_by % 4

    def ag_copy(phase, sub, unit_by, message, where, by):
        block = gathered(phase, sub, unit_by, where)
        return pltpu.make_async_remote_copy(
            src_ref=block, dst_ref=block,
            send_sem=ag_send.at[sub, slot(phase, unit_by), message],
            recv_sem=ag_recv.at[sub, slot(phase, unit_by), message],
            device_id=neighbour(GATHER[sub][0][phase], by), device_id_type=MESH,
        )

    def ag_start(phase, sub, unit_by=0):
        axis, way = GATHER[sub][0][phase], GATHER[sub][1]
        go(ag_copy(phase, sub, unit_by, 0, place[axis], way))
        go(ag_copy(phase, sub, unit_by, 1, place[axis], -way))

    def ag_forward(phase, sub, unit_by=0):
        axis, way = GATHER[sub][0][phase], GATHER[sub][1]
        ag_copy(phase, sub, unit_by, 0, moved(axis, -way), way).wait_recv()
        go(ag_copy(phase, sub, unit_by, 2, moved(axis, -way), way))

    def ag_wait(phase, sub, message, unit_by=0):
        axis, way = GATHER[sub][0][phase], GATHER[sub][1]
        ag_copy(phase, sub, unit_by, message, moved(axis, way if message == 1 else 2), way).wait_recv()

    def plane(order, where):
        index = [slice(None)] * 3
        index[order[2]] = where
        return tuple(index)

    def first_products(sub, by):
        order, way, lo, size = GATHER[sub]
        at = plane(order, moved(order[2], by))
        block = tokens[(*at, slice(None), pl.ds(lo, size))].reshape(256, size)
        above = jnp.dot(block, up[pl.ds(lo, size), :], preferred_element_type=jnp.float32)
        hid[(*at, pl.ds(0, 8), pl.ds(0, HID))] += above.reshape(4, 4, 16, HID)[:, :, :8]
        down = part[lo // HALF, :, :, :, pl.ds(lo % HALF, size)].reshape(HID, size)
        below = lax.dot_general(block, down, (((1,), (1,)), ((), ())), preferred_element_type=jnp.float32)
        hid[(*at, pl.ds(8, 8), pl.ds(HID, HID))] += below.reshape(4, 4, 16, HID)[:, :, 8:]

    def way_of(sub):
        return GATHER[sub][1]

    for sub in SUBS:
        ag_start(0, sub)
    for sub in SUBS:
        ag_start(1, sub, 0)
    load_up = pltpu.make_async_copy(up_hbm, up, load_sem.at[0])
    load_down = [
        pltpu.make_async_copy(down_hbm.at[:, :, :, pl.ds(half * HALF, HALF)], part.at[half], load_sem.at[1 + half])
        for half in range(2)
    ]
    load_up.start()
    for load in load_down:
        load.start()
    hid[...] = jnp.zeros_like(hid)
    for sub in SUBS:
        ag_forward(0, sub)
        ag_start(1, sub, -way_of(sub))
    for sub in SUBS:
        ag_wait(0, sub, 1)
        ag_start(1, sub, way_of(sub))
    for sub in SUBS:
        ag_forward(1, sub, 0)
    for sub in SUBS:
        ag_wait(0, sub, 2)
        ag_start(1, sub, 2)
        ag_start(2, sub, 0)
    for sub in SUBS:
        ag_forward(1, sub, -way_of(sub))
    for sub in SUBS:
        ag_forward(1, sub, way_of(sub))
    for sub in SUBS:
        ag_forward(1, sub, 2)
        ag_start(2, sub, -way_of(sub))
    for sub in SUBS:
        for unit_by in range(4):
            ag_wait(1, sub, 1, unit_by)
        ag_start(2, sub, way_of(sub))
    for sub in SUBS:
        for unit_by in range(4):
            ag_wait(1, sub, 2, unit_by)
        ag_start(2, sub, 2)
    load_up.wait()
    for load in load_down:
        load.wait()
    for sub in SUBS:
        ag_forward(2, sub, 0)
    for sub in SUBS:
        first_products(sub, 0)
    for sub in SUBS:
        ag_forward(2, sub, -way_of(sub))
    for sub in SUBS:
        ag_forward(2, sub, way_of(sub))
    for sub in SUBS:
        ag_forward(2, sub, 2)
    for sub in SUBS:
        first_products(sub, -way_of(sub))
    for sub in SUBS:
        for unit_by in range(4):
            ag_wait(2, sub, 1, unit_by)
        first_products(sub, way_of(sub))
    for sub in SUBS:
        for unit_by in range(4):
            ag_wait(2, sub, 2, unit_by)
        first_products(sub, 2)

    SWAPPED = (0, 2, 1, 3)

    def activate(step, carry):
        z, y = step // 4, step % 4
        act, derivative = gelu_pair(hid[z, y, :, 0:8, 0:HID])
        for x in range(4):
            hid[z, y, x, 0:8, HID:] = hid[y, z, SWAPPED[x], 8:16, HID:] * derivative[x]
            hid[z, y, x, 0:8, 0:HID] = act[x]
        return carry

    lax.fori_loop(0, 16, activate, 0)

    def lay_out(step, carry):
        z, y = step // 4, step % 4
        blank = jnp.zeros((8, HID), jnp.float32)
        for x in range(4):
            weights[z, y, x, :, 0:HID] = jnp.concatenate([hid[z, y, x, 0:8, HID:], blank], axis=0).astype(jnp.bfloat16)
            weights[z, y, x, :, HID:] = jnp.concatenate(
                [blank, hid[y, z, SWAPPED[x], 0:8, 0:HID]], axis=0
            ).astype(jnp.bfloat16)
        return carry

    def second_products(sub, by):
        order, _, lo, size = SCATTER[sub]
        at = plane(order, moved(order[2], by))
        left = hid[(*at, pl.ds(0, 8), pl.ds(HID, HID))].reshape(128, HID).astype(jnp.bfloat16)
        halves = []
        for start in (lo, HALF + lo):
            halves.append(
                lax.dot_general(
                    left, up[pl.ds(start, size), :], (((1,), (1,)), ((), ())), preferred_element_type=jnp.float32
                ).reshape(4, 4, 8, size)
            )
        part[(*at, slice(None), pl.ds(lo, size))] = jnp.concatenate(halves, axis=2).astype(jnp.bfloat16)

    def two_axes(order, b_index, a_index=slice(None)):
        return tuple(b_index if axis == order[1] else a_index for axis in range(3) if axis != order[2])

    def landing(phase, sub, unit_by, message):
        order, _, lo, size = SCATTER[sub]
        columns = (slice(None), pl.ds(lo, size))
        if phase == 0:
            return got0.at[(message, *two_axes(order, moved(order[1], unit_by)), *columns)]
        if phase == 1:
            return got1.at[(message, moved(order[0], unit_by), *columns)]
        return got2.at[(message, *columns)]

    def share(phase, sub, unit_by, by):
        order, _, lo, size = SCATTER[sub]
        columns = (slice(None), pl.ds(lo, size))
        where = moved(order[2 - phase], by)
        if phase == 0:
            index = list(plane(order, where))
            index[order[1]] = moved(order[1], unit_by)
            return part.at[(*index, *columns)]
        if phase == 1:
            return got0.at[(2, *two_axes(order, where, moved(order[0], unit_by)), *columns)]
        return got1.at[(2, where, *columns)]

    def rs_copy(phase, sub, unit_by, message):
        order, way = SCATTER[sub][0], SCATTER[sub][1]
        if message == 0:
            source, by = share(phase, sub, unit_by, 2), -way
        elif message == 1:
            source, by = share(phase, sub, unit_by, way), way
        else:
            source, by = landing(phase, sub, unit_by, 0), -way
        at = slot(2, unit_by) if phase == 0 else slot(1, unit_by) if phase == 1 else 0
        return pltpu.make_async_remote_copy(
            src_ref=source, dst_ref=landing(phase, sub, unit_by, message),
            send_sem=rs_send.at[sub, at, message], recv_sem=rs_recv.at[sub, at, message],
            device_id=neighbour(order[2 - phase], by), device_id_type=MESH,
        )

    def rs_start(phase, sub, unit_by, message):
        go(rs_copy(phase, sub, unit_by, message))

    def rs_forward(phase, sub, unit_by=0):
        rs_copy(phase, sub, unit_by, 0).wait_recv()
        ref = landing(phase, sub, unit_by, 0)
        mine = share(phase, sub, unit_by, -way_of(sub))
        ref[...] = (f32(ref[...]) + f32(mine[...])).astype(jnp.bfloat16)
        rs_start(phase, sub, unit_by, 2)

    def rs_sum(phase, sub, unit_by=0):
        rs_copy(phase, sub, unit_by, 1).wait_recv()
        rs_copy(phase, sub, unit_by, 2).wait_recv()
        mine = share(phase, sub, unit_by, 0)
        ref = landing(phase, sub, unit_by, 2)
        summed = f32(mine[...]) + f32(landing(phase, sub, unit_by, 1)[...]) + f32(ref[...])
        if phase < 2:
            ref[...] = summed.astype(jnp.bfloat16)
        return summed

    def far_first(sub):
        return (2, way_of(sub), -way_of(sub), 0)

    for sub in SUBS:
        second_products(sub, 2)
        for unit_by in far_first(sub):
            rs_start(0, sub, unit_by, 0)
    for sub in SUBS:
        second_products(sub, way_of(sub))
        for unit_by in far_first(sub):
            rs_start(0, sub, unit_by, 1)
    for sub in SUBS:
        second_products(sub, -way_of(sub))
    for turn in range(4):
        for sub in SUBS:
            rs_forward(0, sub, far_first(sub)[turn])
    for sub in SUBS:
        second_products(sub, 0)
    lax.fori_loop(0, 16, lay_out, 0)

    def gain_tile(step, carry):
        at = pl.ds(pl.multiple_of(step * 256, 256), 256)
        also = pl.ds(pl.multiple_of(HALF + step * 256, 256), 256)
        sums = [jnp.zeros((8, 256), jnp.float32)] * 2
        for z in range(4):
            here = f32(part[z, :, :, :, at]).reshape(16, 16, 256)
            for half, columns in enumerate((at, also)):
                rows = f32(tokens[z, :, :, :, columns]).reshape(16, 16, 256)[:, :8]
                sums[half] = sums[half] + jnp.sum(here[:, 8 * half : 8 * half + 8] * rows, axis=0)
        gain_acc[:, at] = sums[0]
        gain_acc[:, also] = sums[1]
        return carry

    lax.fori_loop(0, HALF // 256, gain_tile, 0)
    gain_slots[0, place[2]] = jnp.sum(gain_acc[...], axis=0, keepdims=True) / f32(gain[...])

    def gain_copy(phase, by, owner):
        axis = 2 - phase
        return pltpu.make_async_remote_copy(
            src_ref=gain_slots.at[phase, owner], dst_ref=gain_slots.at[phase, owner],
            send_sem=gain_send.at[phase, by - 1], recv_sem=gain_recv.at[phase, by - 1],
            device_id=neighbour(axis, by), device_id_type=MESH,
        )

    def gain_start(phase):
        for by in (1, 2, 3):
            go(gain_copy(phase, by, place[2 - phase]))

    def gain_sum(phase):
        for by in (1, 2, 3):
            gain_copy(phase, by, moved(2 - phase, -by)).wait_recv()
        return (gain_slots[phase, 0] + gain_slots[phase, 1]) + (gain_slots[phase, 2] + gain_slots[phase, 3])

    TILE = 512

    def weight_tile(step, carry):
        at = pl.ds(pl.multiple_of(step * TILE, TILE), TILE)
        block = tokens[:, :, :, :, at].reshape(1024, TILE)
        up_grad[at, :] = lax.dot_general(
            block, weights[:, :, :, :, 0:HID].reshape(1024, HID), (((0,), (0,)), ((), ())),
            preferred_element_type=jnp.float32,
        )
        down_grad[:, at] = lax.dot_general(
            weights[:, :, :, :, HID:].reshape(1024, HID), block, (((0,), (0,)), ((), ())),
            preferred_element_type=jnp.float32,
        )
        return carry

    gain_start(0)
    lax.fori_loop(0, 8, weight_tile, 0)
    gain_slots[1, place[1]] = gain_sum(0)
    gain_start(1)
    lax.fori_loop(8, 16, weight_tile, 0)
    gain_slots[2, place[0]] = gain_sum(1)
    gain_start(2)

    for sub in SUBS:
        rs_sum(0, sub, 2)
        for unit_by in far_first(sub):
            rs_start(1, sub, unit_by, 0)
    for sub in SUBS:
        rs_sum(0, sub, way_of(sub))
        for unit_by in far_first(sub):
            rs_start(1, sub, unit_by, 1)
    for sub in SUBS:
        rs_sum(0, sub, -way_of(sub))
    for turn in range(4):
        for sub in SUBS:
            rs_forward(1, sub, far_first(sub)[turn])
    for sub in SUBS:
        rs_sum(0, sub, 0)
    gain_grad[...] = gain_sum(2)
    for sub in SUBS:
        rs_sum(1, sub, 2)
        rs_start(2, sub, 0, 0)
    for sub in SUBS:
        rs_sum(1, sub, way_of(sub))
        rs_start(2, sub, 0, 1)
    for sub in SUBS:
        rs_sum(1, sub, -way_of(sub))
    for sub in SUBS:
        rs_forward(2, sub)
    for sub in SUBS:
        rs_sum(1, sub, 0)
    own[...] = f32(tokens[place[1], place[0], (place[2] % 2) * 2 + place[2] // 2])[8:]
    for sub in SUBS:
        _, _, lo, size = SCATTER[sub]
        summed = rs_sum(2, sub)
        total[:, pl.ds(lo, size)] = summed[:8]
        total[:, pl.ds(HALF + lo, size)] = summed[8:]
    for copy in started:
        copy.wait_send()


def finish(
    up_grad, down_grad, total, unit, inverse, own, gain_grad, gain,
    input_out, gain_out, up_out, down_out,
    input_rows, sem,
):
    PIECES = 4
    copies = [pltpu.make_async_copy(gain_grad, gain_out, sem.at[0])]
    for piece in range(PIECES):
        for which, (source, target) in enumerate(((up_grad, up_out), (down_grad, down_out))):
            size = source.shape[0] // PIECES
            at = pl.ds(piece * size, size)
            copies.append(pltpu.make_async_copy(source.at[at, :], target.at[at, :], sem.at[2 + 2 * piece + which]))
    for copy in copies:
        copy.start()

    scaled = total[...] * f32(gain[...])
    units = unit[...]
    inner_mean = jnp.mean(scaled, axis=-1, keepdims=True)
    proj_mean = jnp.mean(scaled * units, axis=-1, keepdims=True)
    change = inverse[:, 0:1] * (scaled - inner_mean - units * proj_mean)
    input_rows[...] = (own[...] + change).astype(jnp.bfloat16)
    copies.append(pltpu.make_async_copy(input_rows, input_out, sem.at[1]))
    copies[-1].start()
    for copy in copies:
        copy.wait()


def on_device(upstream, saved_input, norm_gain, up_weight, down_weight):
    bf16, f4 = jnp.bfloat16, jnp.float32
    vmem, hbm = pl.BlockSpec(memory_space=pltpu.VMEM), pl.BlockSpec(memory_space=pl.ANY)
    dma = pltpu.SemaphoreType.DMA
    held = pl.pallas_call(
        kernel,
        out_shape=[
            pltpu.VMEM((D, HID), f4),
            pltpu.VMEM((HID, D), f4),
            pltpu.VMEM((ROWS, D), f4),
            pltpu.VMEM((ROWS, D), f4),
            pltpu.VMEM((ROWS, 128), f4),
            pltpu.VMEM((ROWS, D), f4),
            pltpu.VMEM((1, D), f4),
        ],
        in_specs=[vmem, vmem, vmem, hbm, hbm],
        out_specs=[vmem] * 7,
        scratch_shapes=[
            pltpu.VMEM((4, 4, 4, 16, D), bf16),
            pltpu.VMEM((4, 4, 4, 16, 2 * HID), bf16),
            pltpu.VMEM((D, HID), bf16),
            pltpu.VMEM((4, 4, 4, 16, HALF), bf16),
            pltpu.VMEM((3, 4, 4, 16, HALF), bf16),
            pltpu.VMEM((3, 4, 16, HALF), bf16),
            pltpu.VMEM((3, 16, HALF), bf16),
            pltpu.VMEM((4, 4, 4, 16, 2 * HID), f4),
            pltpu.VMEM((ROWS, D), f4),
            pltpu.VMEM((ROWS, D), f4),
            pltpu.VMEM((ROWS, D), f4),
            pltpu.VMEM((3, 4, 1, D), f4),
            dma((3,)), dma((2,)),
            dma((6, 9, 3)), dma((6, 9, 3)), dma((6, 9, 3)), dma((6, 9, 3)),
            dma((3, 3)), dma((3, 3)),
        ],
        compiler_params=pltpu.CompilerParams(
            collective_id=0, has_side_effects=True, vmem_limit_bytes=42 * 2**20
        ),
        name="section_backward",
    )(upstream[0], saved_input[0], norm_gain, up_weight[0], down_weight[0].reshape(4, 4, 16, D))
    held = [pltpu.with_memory_space_constraint(array, pltpu.VMEM) for array in held]
    input_grad, gain_grad, up_grad, down_grad = pl.pallas_call(
        finish,
        out_shape=[
            jax.ShapeDtypeStruct((ROWS, D), bf16),
            jax.ShapeDtypeStruct((1, D), f4),
            jax.ShapeDtypeStruct((D, HID), f4),
            jax.ShapeDtypeStruct((HID, D), f4),
        ],
        in_specs=[vmem] * 8,
        out_specs=[hbm] * 4,
        scratch_shapes=[
            pltpu.VMEM((ROWS, D), bf16),
            dma((10,)),
        ],
        compiler_params=pltpu.CompilerParams(vmem_limit_bytes=4 * 2**20),
        name="finish",
    )(*held, norm_gain)
    return (input_grad[None], up_grad[None], down_grad[None], gain_grad)


def solution(mesh):
    in_specs = (
        P("section", ("dp", "tensor"), None),
        P("section", ("dp", "tensor"), None),
        P("section", None),
        P("section", None, ("dp", "tensor")),
        P("section", ("dp", "tensor"), None),
    )
    out_specs = (
        P("section", ("dp", "tensor"), None),
        P("section", None, ("dp", "tensor")),
        P("section", ("dp", "tensor"), None),
        P("section", None),
    )
    return jax.shard_map(
        on_device, mesh=mesh, in_specs=in_specs, out_specs=out_specs, check_vma=False
    )
```

```python
import jax
import jax.numpy as jnp
from jax import lax
from jax.experimental import pallas as pl
from jax.experimental.pallas import tpu as pltpu
from jax.sharding import PartitionSpec as P

gelu_scale = 0.7978845608028654
cubic_coef = 0.044715

D = 8192
HALF = D // 2
HID = 256
ROWS = 8
MESH = pl.DeviceIdType.MESH

ORDERS = ((2, 1, 0), (0, 2, 1), (1, 0, 2))


def cut(tiles):
    subs, at = [], 0
    for number, count in enumerate(tiles):
        subs.append((ORDERS[number // 2], 1 if number % 2 == 0 else -1, at * 128, count * 128))
        at += count
    return tuple(subs)


GATHER = cut((11, 11, 10, 11, 11, 10))
SCATTER = cut((6, 5, 6, 5, 5, 5))
SUBS = range(6)


def gelu_pair(hidden):
    tanh_part = jnp.tanh(gelu_scale * (hidden + cubic_coef * hidden * hidden * hidden))
    gelu_out = 0.5 * hidden * (1.0 + tanh_part)
    derivative = 0.5 * (1.0 + tanh_part) + 0.5 * hidden * (
        1.0 - tanh_part * tanh_part
    ) * gelu_scale * (1.0 + 3.0 * cubic_coef * hidden * hidden)
    return (gelu_out, derivative)


def f32(value):
    return value.astype(jnp.float32)


def apart(blocks, size):
    wide = f32(blocks).reshape(-1, 16, size)
    return tuple(half.reshape(-1, size).astype(jnp.bfloat16) for half in (wide[:, :8], wide[:, 8:]))


def kernel(
    upstream, saved, gain, up_hbm, down_hbm,
    up_grad, down_grad, total, unit, inverse, own, gain_grad,
    tokens, weights, up, part, got0, got1, got2, hid, sent_rows, arrived_rows, gain_acc, gain_slots,
    load_sem, swap_sem, ag_send, ag_recv, rs_send, rs_recv, gain_send, gain_recv,
):
    section = lax.axis_index("section")
    dp = lax.axis_index("dp")
    tensor = lax.axis_index("tensor")
    place = (dp // 2, tensor // 2, (tensor % 2) * 2 + dp % 2)
    started = []

    def go(copy):
        copy.start()
        started.append(copy)

    def device_at(z, y, x):
        return (section, z * 2 + x % 2, y * 2 + x // 2)

    def moved(axis, by):
        return lax.rem(place[axis] + (by + 4), 4)

    def neighbour(axis, by):
        there = list(place)
        there[axis] = moved(axis, by)
        return device_at(*there)

    partner = (1 - section, dp, tensor)

    barrier = pltpu.get_barrier_semaphore()
    others = [neighbour(axis, by) for axis in range(3) for by in (1, 2, 3)] + [partner]
    for other in others:
        pl.semaphore_signal(barrier, inc=1, device_id=other, device_id_type=MESH)
    sent_rows[...] = f32(upstream[...])
    rows = f32(saved[...])
    centered = rows - jnp.mean(rows, axis=-1, keepdims=True)
    spread = lax.rsqrt(jnp.mean(centered * centered, axis=-1, keepdims=True) + 1e-05)
    inverse[...] = jnp.broadcast_to(spread, inverse.shape)
    unit[...] = centered * spread
    pl.semaphore_wait(barrier, len(others))

    swap = pltpu.make_async_remote_copy(
        src_ref=sent_rows, dst_ref=arrived_rows, send_sem=swap_sem.at[0], recv_sem=swap_sem.at[1],
        device_id=partner, device_id_type=MESH,
    )
    go(swap)
    normed = unit[...] * f32(gain[...])
    swap.wait_recv()
    tokens[place[0], place[1], place[2]] = jnp.concatenate([normed, arrived_rows[...]], axis=0).astype(jnp.bfloat16)

    def gathered(phase, sub, unit_by, where):
        order, _, lo, size = GATHER[sub]
        index = [slice(None)] * 3
        for later in range(phase, 3):
            index[order[later]] = place[order[later]]
        if phase:
            index[order[phase - 1]] = moved(order[phase - 1], unit_by)
        index[order[phase]] = where
        return tokens.at[(*index, slice(None), pl.ds(lo, size))]

    def slot(phase, unit_by):
        return 0 if phase == 0 else 4 * phase - 3 + unit_by % 4

    def ag_copy(phase, sub, unit_by, message, where, by):
        block = gathered(phase, sub, unit_by, where)
        return pltpu.make_async_remote_copy(
            src_ref=block, dst_ref=block,
            send_sem=ag_send.at[sub, slot(phase, unit_by), message],
            recv_sem=ag_recv.at[sub, slot(phase, unit_by), message],
            device_id=neighbour(GATHER[sub][0][phase], by), device_id_type=MESH,
        )

    def ag_start(phase, sub, unit_by=0):
        axis, way = GATHER[sub][0][phase], GATHER[sub][1]
        go(ag_copy(phase, sub, unit_by, 0, place[axis], way))
        go(ag_copy(phase, sub, unit_by, 1, place[axis], -way))

    def ag_forward(phase, sub, unit_by=0):
        axis, way = GATHER[sub][0][phase], GATHER[sub][1]
        ag_copy(phase, sub, unit_by, 0, moved(axis, -way), way).wait_recv()
        go(ag_copy(phase, sub, unit_by, 2, moved(axis, -way), way))

    def ag_wait(phase, sub, message, unit_by=0):
        axis, way = GATHER[sub][0][phase], GATHER[sub][1]
        ag_copy(phase, sub, unit_by, message, moved(axis, way if message == 1 else 2), way).wait_recv()

    def plane(order, where):
        index = [slice(None)] * 3
        index[order[2]] = where
        return tuple(index)

    def first_products(sub, by):
        order, way, lo, size = GATHER[sub]
        at = plane(order, moved(order[2], by))
        above, below = apart(tokens[(*at, slice(None), pl.ds(lo, size))], size)
        above = jnp.dot(above, up[pl.ds(lo, size), :], preferred_element_type=jnp.float32)
        hid[(*at, pl.ds(0, 8), pl.ds(0, HID))] += above.reshape(4, 4, 8, HID)
        down = part[lo // HALF, :, :, :, pl.ds(lo % HALF, size)].reshape(HID, size)
        below = lax.dot_general(below, down, (((1,), (1,)), ((), ())), preferred_element_type=jnp.float32)
        hid[(*at, pl.ds(8, 8), pl.ds(HID, HID))] += below.reshape(4, 4, 8, HID)

    def way_of(sub):
        return GATHER[sub][1]

    for sub in SUBS:
        ag_start(0, sub)
    for sub in SUBS:
        ag_start(1, sub, 0)
    load_up = pltpu.make_async_copy(up_hbm, up, load_sem.at[0])
    load_down = [
        pltpu.make_async_copy(down_hbm.at[:, :, :, pl.ds(half * HALF, HALF)], part.at[half], load_sem.at[1 + half])
        for half in range(2)
    ]
    load_up.start()
    for load in load_down:
        load.start()
    hid[...] = jnp.zeros_like(hid)
    for sub in SUBS:
        ag_forward(0, sub)
        ag_start(1, sub, -way_of(sub))
    for sub in SUBS:
        ag_wait(0, sub, 1)
        ag_start(1, sub, way_of(sub))
    for sub in SUBS:
        ag_forward(1, sub, 0)
    for sub in SUBS:
        ag_wait(0, sub, 2)
        ag_start(1, sub, 2)
        ag_start(2, sub, 0)
    for sub in SUBS:
        ag_forward(1, sub, -way_of(sub))
    for sub in SUBS:
        ag_forward(1, sub, way_of(sub))
    for sub in SUBS:
        ag_forward(1, sub, 2)
        ag_start(2, sub, -way_of(sub))
    for sub in SUBS:
        for unit_by in range(4):
            ag_wait(1, sub, 1, unit_by)
        ag_start(2, sub, way_of(sub))
    for sub in SUBS:
        for unit_by in range(4):
            ag_wait(1, sub, 2, unit_by)
        ag_start(2, sub, 2)
    load_up.wait()
    for load in load_down:
        load.wait()
    for sub in SUBS:
        ag_forward(2, sub, 0)
    for sub in SUBS:
        first_products(sub, 0)
    for sub in SUBS:
        ag_forward(2, sub, -way_of(sub))
    for sub in SUBS:
        ag_forward(2, sub, way_of(sub))
    for sub in SUBS:
        ag_forward(2, sub, 2)
    for sub in SUBS:
        first_products(sub, -way_of(sub))
    for sub in SUBS:
        for unit_by in range(4):
            ag_wait(2, sub, 1, unit_by)
        first_products(sub, way_of(sub))
    for sub in SUBS:
        for unit_by in range(4):
            ag_wait(2, sub, 2, unit_by)
        first_products(sub, 2)

    SWAPPED = (0, 2, 1, 3)

    def activate(step, carry):
        z, y = step // 4, step % 4
        act, derivative = gelu_pair(hid[z, y, :, 0:8, 0:HID])
        for x in range(4):
            hid[z, y, x, 0:8, HID:] = hid[y, z, SWAPPED[x], 8:16, HID:] * derivative[x]
            hid[z, y, x, 0:8, 0:HID] = act[x]
        return carry

    lax.fori_loop(0, 16, activate, 0)

    def lay_out(step, carry):
        z, y = step // 4, step % 4
        for pair in range(2):
            first, second = 2 * pair, 2 * pair + 1
            weights[0, z, y, pair] = jnp.concatenate(
                [hid[z, y, x, 0:8, HID:] for x in (first, second)], axis=0
            ).astype(jnp.bfloat16)
            weights[1, z, y, pair] = jnp.concatenate(
                [hid[y, z, SWAPPED[x], 0:8, 0:HID] for x in (first, second)], axis=0
            ).astype(jnp.bfloat16)
        return carry

    def second_products(sub, by):
        order, _, lo, size = SCATTER[sub]
        at = plane(order, moved(order[2], by))
        left = hid[(*at, pl.ds(0, 8), pl.ds(HID, HID))].reshape(128, HID).astype(jnp.bfloat16)
        halves = []
        for start in (lo, HALF + lo):
            halves.append(
                lax.dot_general(
                    left, up[pl.ds(start, size), :], (((1,), (1,)), ((), ())), preferred_element_type=jnp.float32
                ).reshape(4, 4, 8, size)
            )
        part[(*at, slice(None), pl.ds(lo, size))] = jnp.concatenate(halves, axis=2).astype(jnp.bfloat16)

    def two_axes(order, b_index, a_index=slice(None)):
        return tuple(b_index if axis == order[1] else a_index for axis in range(3) if axis != order[2])

    def landing(phase, sub, unit_by, message):
        order, _, lo, size = SCATTER[sub]
        columns = (slice(None), pl.ds(lo, size))
        if phase == 0:
            return got0.at[(message, *two_axes(order, moved(order[1], unit_by)), *columns)]
        if phase == 1:
            return got1.at[(message, moved(order[0], unit_by), *columns)]
        return got2.at[(message, *columns)]

    def share(phase, sub, unit_by, by):
        order, _, lo, size = SCATTER[sub]
        columns = (slice(None), pl.ds(lo, size))
        where = moved(order[2 - phase], by)
        if phase == 0:
            index = list(plane(order, where))
            index[order[1]] = moved(order[1], unit_by)
            return part.at[(*index, *columns)]
        if phase == 1:
            return got0.at[(2, *two_axes(order, where, moved(order[0], unit_by)), *columns)]
        return got1.at[(2, where, *columns)]

    def rs_copy(phase, sub, unit_by, message):
        order, way = SCATTER[sub][0], SCATTER[sub][1]
        if message == 0:
            source, by = share(phase, sub, unit_by, 2), -way
        elif message == 1:
            source, by = share(phase, sub, unit_by, way), way
        else:
            source, by = landing(phase, sub, unit_by, 0), -way
        at = slot(2, unit_by) if phase == 0 else slot(1, unit_by) if phase == 1 else 0
        return pltpu.make_async_remote_copy(
            src_ref=source, dst_ref=landing(phase, sub, unit_by, message),
            send_sem=rs_send.at[sub, at, message], recv_sem=rs_recv.at[sub, at, message],
            device_id=neighbour(order[2 - phase], by), device_id_type=MESH,
        )

    def rs_start(phase, sub, unit_by, message):
        go(rs_copy(phase, sub, unit_by, message))

    def rs_forward(phase, sub, unit_by=0):
        rs_copy(phase, sub, unit_by, 0).wait_recv()
        ref = landing(phase, sub, unit_by, 0)
        mine = share(phase, sub, unit_by, -way_of(sub))
        ref[...] = (f32(ref[...]) + f32(mine[...])).astype(jnp.bfloat16)
        rs_start(phase, sub, unit_by, 2)

    def rs_sum(phase, sub, unit_by=0):
        rs_copy(phase, sub, unit_by, 1).wait_recv()
        rs_copy(phase, sub, unit_by, 2).wait_recv()
        mine = share(phase, sub, unit_by, 0)
        ref = landing(phase, sub, unit_by, 2)
        summed = f32(mine[...]) + f32(landing(phase, sub, unit_by, 1)[...]) + f32(ref[...])
        if phase < 2:
            ref[...] = summed.astype(jnp.bfloat16)
        return summed

    def far_first(sub):
        return (2, way_of(sub), -way_of(sub), 0)

    for sub in SUBS:
        second_products(sub, 2)
        for turn in (0, 1):
            rs_start(0, sub, far_first(sub)[turn], 0)
    for sub in SUBS:
        second_products(sub, way_of(sub))
        rs_start(0, sub, far_first(sub)[0], 1)
    for sub in SUBS:
        second_products(sub, -way_of(sub))

    def line_step(turn):
        for sub in SUBS:
            rs_forward(0, sub, far_first(sub)[turn])
            if turn < 2:
                rs_start(0, sub, far_first(sub)[turn + 2], 0)
            if turn < 3:
                rs_start(0, sub, far_first(sub)[turn + 1], 1)

    def line_sum(turn):
        for sub in SUBS:
            rs_sum(0, sub, far_first(sub)[turn])
            if turn < 2:
                for unit_by in far_first(sub):
                    rs_start(1, sub, unit_by, turn)

    line_step(0)
    lax.fori_loop(0, 16, lay_out, 0)
    line_step(1)
    for sub in SUBS:
        second_products(sub, 0)
    line_sum(0)
    line_step(2)

    def gain_tile(step, carry):
        at = pl.ds(pl.multiple_of(step * 256, 256), 256)
        also = pl.ds(pl.multiple_of(HALF + step * 256, 256), 256)
        sums = [jnp.zeros((8, 256), jnp.float32)] * 2
        for z in range(4):
            here = f32(part[z, :, :, :, at]).reshape(16, 16, 256)
            for half, columns in enumerate((at, also)):
                rows = f32(tokens[z, :, :, :, columns]).reshape(16, 16, 256)[:, :8]
                sums[half] = sums[half] + jnp.sum(here[:, 8 * half : 8 * half + 8] * rows, axis=0)
        gain_acc[:, at] = sums[0]
        gain_acc[:, also] = sums[1]
        return carry

    lax.fori_loop(0, HALF // 256, gain_tile, 0)
    gain_slots[0, place[2]] = jnp.sum(gain_acc[...], axis=0, keepdims=True) / f32(gain[...])

    def gain_copy(phase, by, owner):
        axis = 2 - phase
        return pltpu.make_async_remote_copy(
            src_ref=gain_slots.at[phase, owner], dst_ref=gain_slots.at[phase, owner],
            send_sem=gain_send.at[phase, by - 1], recv_sem=gain_recv.at[phase, by - 1],
            device_id=neighbour(axis, by), device_id_type=MESH,
        )

    def gain_start(phase):
        for by in (1, 2, 3):
            go(gain_copy(phase, by, place[2 - phase]))

    def gain_sum(phase):
        for by in (1, 2, 3):
            gain_copy(phase, by, moved(2 - phase, -by)).wait_recv()
        return (gain_slots[phase, 0] + gain_slots[phase, 1]) + (gain_slots[phase, 2] + gain_slots[phase, 3])

    TILE = 512

    def weight_tile(step, carry):
        at = pl.ds(pl.multiple_of(step * TILE, TILE), TILE)
        above, below = apart(tokens[:, :, :, :, at], TILE)
        up_grad[at, :] = lax.dot_general(
            above, weights[0].reshape(512, HID), (((0,), (0,)), ((), ())), preferred_element_type=jnp.float32
        )
        down_grad[:, at] = lax.dot_general(
            weights[1].reshape(512, HID), below, (((0,), (0,)), ((), ())), preferred_element_type=jnp.float32
        )
        return carry

    gain_start(0)
    line_sum(1)
    line_step(3)
    lax.fori_loop(0, 6, weight_tile, 0)
    gain_slots[1, place[1]] = gain_sum(0)
    gain_start(1)
    line_sum(2)
    for turn in range(4):
        for sub in SUBS:
            rs_forward(1, sub, far_first(sub)[turn])
    lax.fori_loop(6, 12, weight_tile, 0)
    gain_slots[2, place[0]] = gain_sum(1)
    gain_start(2)
    line_sum(3)
    for turn in (0, 1):
        for sub in SUBS:
            rs_sum(1, sub, far_first(sub)[turn])
            rs_start(2, sub, 0, turn)
    lax.fori_loop(12, 16, weight_tile, 0)
    for sub in SUBS:
        rs_sum(1, sub, -way_of(sub))
    for sub in SUBS:
        rs_forward(2, sub)
    for sub in SUBS:
        rs_sum(1, sub, 0)
    gain_grad[...] = gain_sum(2)
    own[...] = f32(tokens[place[1], place[0], (place[2] % 2) * 2 + place[2] // 2])[8:]
    for sub in SUBS:
        _, _, lo, size = SCATTER[sub]
        summed = rs_sum(2, sub)
        total[:, pl.ds(lo, size)] = summed[:8]
        total[:, pl.ds(HALF + lo, size)] = summed[8:]
    for copy in started:
        copy.wait_send()


def finish(
    up_grad, down_grad, total, unit, inverse, own, gain_grad, gain,
    input_out, gain_out, up_out, down_out,
    input_rows, sem,
):
    PIECES = 4
    copies = [pltpu.make_async_copy(gain_grad, gain_out, sem.at[0])]
    for piece in range(PIECES):
        for which, (source, target) in enumerate(((up_grad, up_out), (down_grad, down_out))):
            size = source.shape[0] // PIECES
            at = pl.ds(piece * size, size)
            copies.append(pltpu.make_async_copy(source.at[at, :], target.at[at, :], sem.at[2 + 2 * piece + which]))
    for copy in copies:
        copy.start()

    scaled = total[...] * f32(gain[...])
    units = unit[...]
    inner_mean = jnp.mean(scaled, axis=-1, keepdims=True)
    proj_mean = jnp.mean(scaled * units, axis=-1, keepdims=True)
    change = inverse[:, 0:1] * (scaled - inner_mean - units * proj_mean)
    input_rows[...] = (own[...] + change).astype(jnp.bfloat16)
    copies.append(pltpu.make_async_copy(input_rows, input_out, sem.at[1]))
    copies[-1].start()
    for copy in copies:
        copy.wait()


def on_device(upstream, saved_input, norm_gain, up_weight, down_weight):
    bf16, f4 = jnp.bfloat16, jnp.float32
    vmem, hbm = pl.BlockSpec(memory_space=pltpu.VMEM), pl.BlockSpec(memory_space=pl.ANY)
    dma = pltpu.SemaphoreType.DMA
    held = pl.pallas_call(
        kernel,
        out_shape=[
            pltpu.VMEM((D, HID), f4),
            pltpu.VMEM((HID, D), f4),
            pltpu.VMEM((ROWS, D), f4),
            pltpu.VMEM((ROWS, D), f4),
            pltpu.VMEM((ROWS, 128), f4),
            pltpu.VMEM((ROWS, D), f4),
            pltpu.VMEM((1, D), f4),
        ],
        in_specs=[vmem, vmem, vmem, hbm, hbm],
        out_specs=[vmem] * 7,
        scratch_shapes=[
            pltpu.VMEM((4, 4, 4, 16, D), bf16),
            pltpu.VMEM((2, 4, 4, 2, 16, HID), bf16),
            pltpu.VMEM((D, HID), bf16),
            pltpu.VMEM((4, 4, 4, 16, HALF), bf16),
            pltpu.VMEM((3, 4, 4, 16, HALF), bf16),
            pltpu.VMEM((3, 4, 16, HALF), bf16),
            pltpu.VMEM((3, 16, HALF), bf16),
            pltpu.VMEM((4, 4, 4, 16, 2 * HID), f4),
            pltpu.VMEM((ROWS, D), f4),
            pltpu.VMEM((ROWS, D), f4),
            pltpu.VMEM((ROWS, D), f4),
            pltpu.VMEM((3, 4, 1, D), f4),
            dma((3,)), dma((2,)),
            dma((6, 9, 3)), dma((6, 9, 3)), dma((6, 9, 3)), dma((6, 9, 3)),
            dma((3, 3)), dma((3, 3)),
        ],
        compiler_params=pltpu.CompilerParams(
            collective_id=0, has_side_effects=True, vmem_limit_bytes=42 * 2**20
        ),
        name="section_backward",
    )(upstream[0], saved_input[0], norm_gain, up_weight[0], down_weight[0].reshape(4, 4, 16, D))
    held = [pltpu.with_memory_space_constraint(array, pltpu.VMEM) for array in held]
    input_grad, gain_grad, up_grad, down_grad = pl.pallas_call(
        finish,
        out_shape=[
            jax.ShapeDtypeStruct((ROWS, D), bf16),
            jax.ShapeDtypeStruct((1, D), f4),
            jax.ShapeDtypeStruct((D, HID), f4),
            jax.ShapeDtypeStruct((HID, D), f4),
        ],
        in_specs=[vmem] * 8,
        out_specs=[hbm] * 4,
        scratch_shapes=[
            pltpu.VMEM((ROWS, D), bf16),
            dma((10,)),
        ],
        compiler_params=pltpu.CompilerParams(vmem_limit_bytes=4 * 2**20),
        name="finish",
    )(*held, norm_gain)
    return (input_grad[None], up_grad[None], down_grad[None], gain_grad)


def solution(mesh):
    in_specs = (
        P("section", ("dp", "tensor"), None),
        P("section", ("dp", "tensor"), None),
        P("section", None),
        P("section", None, ("dp", "tensor")),
        P("section", ("dp", "tensor"), None),
    )
    out_specs = (
        P("section", ("dp", "tensor"), None),
        P("section", None, ("dp", "tensor")),
        P("section", ("dp", "tensor"), None),
        P("section", None),
    )
    return jax.shard_map(
        on_device, mesh=mesh, in_specs=in_specs, out_specs=out_specs, check_vma=False
    )
```

```python
import jax
import jax.numpy as jnp
from jax import lax
from jax.experimental import pallas as pl
from jax.experimental.pallas import tpu as pltpu
from jax.sharding import PartitionSpec as P

gelu_scale = 0.7978845608028654
cubic_coef = 0.044715

D = 8192
HALF = D // 2
HID = 256
ROWS = 8
MESH = pl.DeviceIdType.MESH

ORDERS = ((2, 1, 0), (0, 2, 1), (1, 0, 2))


def cut(tiles):
    subs, at = [], 0
    for number, count in enumerate(tiles):
        subs.append((ORDERS[number // 2], 1 if number % 2 == 0 else -1, at * 128, count * 128))
        at += count
    return tuple(subs)


GATHER = cut((11, 11, 10, 11, 11, 10))
SCATTER = cut((6, 5, 6, 5, 5, 5))
SUBS = range(6)


def gelu_pair(hidden):
    tanh_part = jnp.tanh(gelu_scale * (hidden + cubic_coef * hidden * hidden * hidden))
    gelu_out = 0.5 * hidden * (1.0 + tanh_part)
    derivative = 0.5 * (1.0 + tanh_part) + 0.5 * hidden * (
        1.0 - tanh_part * tanh_part
    ) * gelu_scale * (1.0 + 3.0 * cubic_coef * hidden * hidden)
    return (gelu_out, derivative)


def f32(value):
    return value.astype(jnp.float32)


def apart(blocks, size):
    wide = f32(blocks).reshape(-1, 16, size)
    return tuple(half.reshape(-1, size).astype(jnp.bfloat16) for half in (wide[:, :8], wide[:, 8:]))


def kernel(
    upstream, saved, gain, up_hbm, down_hbm,
    up_grad, down_grad, total, unit, inverse, own, gain_grad,
    tokens, weights, up, part, got0, got1, got2, hid, sent_rows, arrived_rows, gain_acc, gain_slots,
    load_sem, swap_sem, ag_send, ag_recv, rs_send, rs_recv, gain_send, gain_recv,
):
    section = lax.axis_index("section")
    dp = lax.axis_index("dp")
    tensor = lax.axis_index("tensor")
    place = (dp // 2, tensor // 2, (tensor % 2) * 2 + dp % 2)
    started = []

    def go(copy):
        copy.start()
        started.append(copy)

    def device_at(z, y, x):
        return (section, z * 2 + x % 2, y * 2 + x // 2)

    def moved(axis, by):
        return lax.rem(place[axis] + (by + 4), 4)

    def neighbour(axis, by):
        there = list(place)
        there[axis] = moved(axis, by)
        return device_at(*there)

    partner = (1 - section, dp, tensor)

    barrier = pltpu.get_barrier_semaphore()
    others = [neighbour(axis, by) for axis in range(3) for by in (1, 2, 3)] + [partner]
    for other in others:
        pl.semaphore_signal(barrier, inc=1, device_id=other, device_id_type=MESH)
    sent_rows[...] = f32(upstream[...])
    rows = f32(saved[...])
    centered = rows - jnp.mean(rows, axis=-1, keepdims=True)
    spread = lax.rsqrt(jnp.mean(centered * centered, axis=-1, keepdims=True) + 1e-05)
    inverse[...] = jnp.broadcast_to(spread, inverse.shape)
    unit[...] = centered * spread
    pl.semaphore_wait(barrier, len(others))

    swap = pltpu.make_async_remote_copy(
        src_ref=sent_rows, dst_ref=arrived_rows, send_sem=swap_sem.at[0], recv_sem=swap_sem.at[1],
        device_id=partner, device_id_type=MESH,
    )
    go(swap)
    normed = unit[...] * f32(gain[...])
    swap.wait_recv()
    tokens[place[0], place[1], place[2]] = jnp.concatenate([normed, arrived_rows[...]], axis=0).astype(jnp.bfloat16)

    def gathered(phase, sub, unit_by, where):
        order, _, lo, size = GATHER[sub]
        index = [slice(None)] * 3
        for later in range(phase, 3):
            index[order[later]] = place[order[later]]
        if phase:
            index[order[phase - 1]] = moved(order[phase - 1], unit_by)
        index[order[phase]] = where
        return tokens.at[(*index, slice(None), pl.ds(lo, size))]

    def slot(phase, unit_by):
        return 0 if phase == 0 else 4 * phase - 3 + unit_by % 4

    def ag_copy(phase, sub, unit_by, message, where, by):
        block = gathered(phase, sub, unit_by, where)
        return pltpu.make_async_remote_copy(
            src_ref=block, dst_ref=block,
            send_sem=ag_send.at[sub, slot(phase, unit_by), message],
            recv_sem=ag_recv.at[sub, slot(phase, unit_by), message],
            device_id=neighbour(GATHER[sub][0][phase], by), device_id_type=MESH,
        )

    def ag_start(phase, sub, unit_by=0):
        axis, way = GATHER[sub][0][phase], GATHER[sub][1]
        go(ag_copy(phase, sub, unit_by, 0, place[axis], way))
        go(ag_copy(phase, sub, unit_by, 1, place[axis], -way))

    def ag_forward(phase, sub, unit_by=0):
        axis, way = GATHER[sub][0][phase], GATHER[sub][1]
        ag_copy(phase, sub, unit_by, 0, moved(axis, -way), way).wait_recv()
        go(ag_copy(phase, sub, unit_by, 2, moved(axis, -way), way))

    def ag_wait(phase, sub, message, unit_by=0):
        axis, way = GATHER[sub][0][phase], GATHER[sub][1]
        ag_copy(phase, sub, unit_by, message, moved(axis, way if message == 1 else 2), way).wait_recv()

    def plane(order, where):
        index = [slice(None)] * 3
        index[order[2]] = where
        return tuple(index)

    def first_products(number, by, lines=None):
        subs = (2 * number, 2 * number + 1)
        order, _, lo, _ = GATHER[subs[0]]
        size = GATHER[subs[0]][3] + GATHER[subs[1]][3]
        places = []
        for line in (None,) if lines is None else lines:
            at = list(plane(order, moved(order[2], by)))
            if line is not None:
                at[order[1]] = moved(order[1], line)
            places.append(tuple(at))
        blocks = [tokens[(*at, slice(None), pl.ds(lo, size))].reshape(-1, 16, size) for at in places]
        above, below = apart(blocks[0] if len(blocks) == 1 else jnp.concatenate(blocks, axis=0), size)
        above = jnp.dot(above, up[pl.ds(lo, size), :], preferred_element_type=jnp.float32)
        sums = []
        for sub in subs:
            start, width = GATHER[sub][2], GATHER[sub][3]
            down = part[start // HALF, :, :, :, pl.ds(start % HALF, width)].reshape(HID, width)
            sums.append(
                lax.dot_general(
                    below[:, start - lo : start - lo + width], down, (((1,), (1,)), ((), ())),
                    preferred_element_type=jnp.float32,
                )
            )
        below = sums[0] + sums[1]
        rows = above.shape[0] // len(places)
        shape = ((4, 4) if lines is None else (4,)) + (8, HID)
        for turn, at in enumerate(places):
            some = slice(turn * rows, (turn + 1) * rows)
            hid[(*at, pl.ds(0, 8), pl.ds(0, HID))] += above[some].reshape(shape)
            hid[(*at, pl.ds(8, 8), pl.ds(HID, HID))] += below[some].reshape(shape)

    def way_of(sub):
        return GATHER[sub][1]

    for sub in SUBS:
        ag_start(0, sub)
    for sub in SUBS:
        ag_start(1, sub, 0)
    load_up = pltpu.make_async_copy(up_hbm, up, load_sem.at[0])
    load_down = [
        pltpu.make_async_copy(down_hbm.at[:, :, :, pl.ds(half * HALF, HALF)], part.at[half], load_sem.at[1 + half])
        for half in range(2)
    ]
    load_up.start()
    for load in load_down:
        load.start()
    hid[...] = jnp.zeros_like(hid)
    for sub in SUBS:
        ag_forward(0, sub)
        ag_start(1, sub, -way_of(sub))
    for sub in SUBS:
        ag_wait(0, sub, 1)
        ag_start(1, sub, way_of(sub))
    for sub in SUBS:
        ag_forward(1, sub, 0)
    for sub in SUBS:
        ag_wait(0, sub, 2)
        ag_start(1, sub, 2)
        ag_start(2, sub, 0)
    for sub in SUBS:
        ag_forward(1, sub, -way_of(sub))
    for sub in SUBS:
        ag_forward(1, sub, way_of(sub))
    for sub in SUBS:
        ag_forward(1, sub, 2)
        ag_start(2, sub, -way_of(sub))
    for sub in SUBS:
        for unit_by in range(4):
            ag_wait(1, sub, 1, unit_by)
        ag_start(2, sub, way_of(sub))
    for sub in SUBS:
        for unit_by in range(4):
            ag_wait(1, sub, 2, unit_by)
        ag_start(2, sub, 2)
    load_up.wait()
    for load in load_down:
        load.wait()
    for sub in SUBS:
        ag_forward(2, sub, 0)
    for number in range(3):
        first_products(number, 0)
    for sub in SUBS:
        ag_forward(2, sub, -way_of(sub))
    for sub in SUBS:
        ag_forward(2, sub, way_of(sub))
    for sub in SUBS:
        ag_forward(2, sub, 2)
    for number in range(3):
        for sub in (2 * number, 2 * number + 1):
            for unit_by in range(4):
                ag_wait(2, sub, 1, unit_by)
        first_products(number, 1)
        first_products(number, -1)
    for unit_by in (0, 1, 3):
        for sub in SUBS:
            ag_wait(2, sub, 2, unit_by)
    for number in range(3):
        first_products(number, 2, (0, 1, -1))
    for number in range(3):
        for sub in (2 * number, 2 * number + 1):
            ag_wait(2, sub, 2, 2)
        first_products(number, 2, (2,))

    SWAPPED = (0, 2, 1, 3)

    def activate(step, carry):
        z, y = step // 4, step % 4
        act, derivative = gelu_pair(hid[z, y, :, 0:8, 0:HID])
        for x in range(4):
            hid[z, y, x, 0:8, HID:] = hid[y, z, SWAPPED[x], 8:16, HID:] * derivative[x]
            hid[z, y, x, 0:8, 0:HID] = act[x]
        return carry

    lax.fori_loop(0, 16, activate, 0)

    def lay_out(step, carry):
        z, y = step // 4, step % 4
        for pair in range(2):
            first, second = 2 * pair, 2 * pair + 1
            weights[0, z, y, pair] = jnp.concatenate(
                [hid[z, y, x, 0:8, HID:] for x in (first, second)], axis=0
            ).astype(jnp.bfloat16)
            weights[1, z, y, pair] = jnp.concatenate(
                [hid[y, z, SWAPPED[x], 0:8, 0:HID] for x in (first, second)], axis=0
            ).astype(jnp.bfloat16)
        return carry

    def second_products(sub, by):
        order, _, lo, size = SCATTER[sub]
        at = plane(order, moved(order[2], by))
        left = hid[(*at, pl.ds(0, 8), pl.ds(HID, HID))].reshape(128, HID).astype(jnp.bfloat16)
        halves = []
        for start in (lo, HALF + lo):
            halves.append(
                lax.dot_general(
                    left, up[pl.ds(start, size), :], (((1,), (1,)), ((), ())), preferred_element_type=jnp.float32
                ).reshape(4, 4, 8, size)
            )
        part[(*at, slice(None), pl.ds(lo, size))] = jnp.concatenate(halves, axis=2).astype(jnp.bfloat16)

    def two_axes(order, b_index, a_index=slice(None)):
        return tuple(b_index if axis == order[1] else a_index for axis in range(3) if axis != order[2])

    def landing(phase, sub, unit_by, message):
        order, _, lo, size = SCATTER[sub]
        columns = (slice(None), pl.ds(lo, size))
        if phase == 0:
            return got0.at[(message, *two_axes(order, moved(order[1], unit_by)), *columns)]
        return got1.at[(message, moved(order[0], unit_by), *columns)]

    def share(phase, sub, unit_by, by):
        order, _, lo, size = SCATTER[sub]
        columns = (slice(None), pl.ds(lo, size))
        where = moved(order[2 - phase], by)
        if phase == 0:
            index = list(plane(order, where))
            index[order[1]] = moved(order[1], unit_by)
            return part.at[(*index, *columns)]
        return got0.at[(2, *two_axes(order, where, moved(order[0], unit_by)), *columns)]

    def rs_copy(phase, sub, unit_by, message):
        order, way = SCATTER[sub][0], SCATTER[sub][1]
        if message == 0:
            source, by = share(phase, sub, unit_by, 2), -way
        elif message == 1:
            source, by = share(phase, sub, unit_by, way), way
        else:
            source, by = landing(phase, sub, unit_by, 0), -way
        at = slot(2 - phase, unit_by)
        return pltpu.make_async_remote_copy(
            src_ref=source, dst_ref=landing(phase, sub, unit_by, message),
            send_sem=rs_send.at[sub, at, message], recv_sem=rs_recv.at[sub, at, message],
            device_id=neighbour(order[2 - phase], by), device_id_type=MESH,
        )

    def rs_start(phase, sub, unit_by, message):
        go(rs_copy(phase, sub, unit_by, message))

    def rs_forward(phase, sub, unit_by=0):
        rs_copy(phase, sub, unit_by, 0).wait_recv()
        ref = landing(phase, sub, unit_by, 0)
        mine = share(phase, sub, unit_by, -way_of(sub))
        ref[...] = (f32(ref[...]) + f32(mine[...])).astype(jnp.bfloat16)
        rs_start(phase, sub, unit_by, 2)

    def rs_sum(phase, sub, unit_by=0):
        rs_copy(phase, sub, unit_by, 1).wait_recv()
        rs_copy(phase, sub, unit_by, 2).wait_recv()
        mine = share(phase, sub, unit_by, 0)
        ref = landing(phase, sub, unit_by, 2)
        summed = f32(mine[...]) + f32(landing(phase, sub, unit_by, 1)[...]) + f32(ref[...])
        ref[...] = summed.astype(jnp.bfloat16)

    def last_copy(sub, by):
        order, _, lo, size = SCATTER[sub]
        columns = (slice(None), pl.ds(lo, size))
        return pltpu.make_async_remote_copy(
            src_ref=got1.at[(2, moved(order[0], by), *columns)], dst_ref=got2.at[(by - 1, *columns)],
            send_sem=rs_send.at[sub, 0, by - 1], recv_sem=rs_recv.at[sub, 0, by - 1],
            device_id=neighbour(order[0], by), device_id_type=MESH,
        )

    def far_first(sub):
        return (2, way_of(sub), -way_of(sub), 0)

    for sub in SUBS:
        second_products(sub, 2)
        for turn in (0, 1):
            rs_start(0, sub, far_first(sub)[turn], 0)
    for sub in SUBS:
        second_products(sub, way_of(sub))
        for turn in (0, 1):
            rs_start(0, sub, far_first(sub)[turn], 1)
    for sub in SUBS:
        second_products(sub, -way_of(sub))

    def line_step(turn):
        for sub in SUBS:
            rs_forward(0, sub, far_first(sub)[turn])
            if turn < 2:
                rs_start(0, sub, far_first(sub)[turn + 2], 0)
            if 0 < turn < 3:
                rs_start(0, sub, far_first(sub)[turn + 1], 1)

    def line_sum(turn):
        for sub in SUBS:
            rs_sum(0, sub, far_first(sub)[turn])
            if turn < 2:
                for unit_by in far_first(sub):
                    rs_start(1, sub, unit_by, turn)

    line_step(0)
    lax.fori_loop(0, 16, lay_out, 0)
    line_step(1)
    for sub in SUBS:
        second_products(sub, 0)
    line_sum(0)
    line_step(2)

    def gain_tile(step, carry):
        at = pl.ds(pl.multiple_of(step * 256, 256), 256)
        also = pl.ds(pl.multiple_of(HALF + step * 256, 256), 256)
        sums = [jnp.zeros((8, 256), jnp.float32)] * 2
        for z in range(4):
            here = f32(part[z, :, :, :, at]).reshape(16, 16, 256)
            for half, columns in enumerate((at, also)):
                rows = f32(tokens[z, :, :, :, columns]).reshape(16, 16, 256)[:, :8]
                sums[half] = sums[half] + jnp.sum(here[:, 8 * half : 8 * half + 8] * rows, axis=0)
        gain_acc[:, at] = sums[0]
        gain_acc[:, also] = sums[1]
        return carry

    lax.fori_loop(0, HALF // 256, gain_tile, 0)
    gain_slots[0, place[2]] = jnp.sum(gain_acc[...], axis=0, keepdims=True) / f32(gain[...])

    def gain_copy(phase, by, owner):
        axis = 2 - phase
        return pltpu.make_async_remote_copy(
            src_ref=gain_slots.at[phase, owner], dst_ref=gain_slots.at[phase, owner],
            send_sem=gain_send.at[phase, by - 1], recv_sem=gain_recv.at[phase, by - 1],
            device_id=neighbour(axis, by), device_id_type=MESH,
        )

    def gain_start(phase):
        for by in (1, 2, 3):
            go(gain_copy(phase, by, place[2 - phase]))

    def gain_sum(phase):
        for by in (1, 2, 3):
            gain_copy(phase, by, moved(2 - phase, -by)).wait_recv()
        return (gain_slots[phase, 0] + gain_slots[phase, 1]) + (gain_slots[phase, 2] + gain_slots[phase, 3])

    TILE = 512

    def weight_tile(step, carry):
        at = pl.ds(pl.multiple_of(step * TILE, TILE), TILE)
        above, below = apart(tokens[:, :, :, :, at], TILE)
        up_grad[at, :] = lax.dot_general(
            above, weights[0].reshape(512, HID), (((0,), (0,)), ((), ())), preferred_element_type=jnp.float32
        )
        down_grad[:, at] = lax.dot_general(
            weights[1].reshape(512, HID), below, (((0,), (0,)), ((), ())), preferred_element_type=jnp.float32
        )
        return carry

    gain_start(0)
    line_sum(1)
    line_step(3)
    lax.fori_loop(0, 6, weight_tile, 0)
    gain_slots[1, place[1]] = gain_sum(0)
    gain_start(1)
    line_sum(2)
    for turn in range(4):
        for sub in SUBS:
            rs_forward(1, sub, far_first(sub)[turn])
    lax.fori_loop(6, 13, weight_tile, 0)
    gain_slots[2, place[0]] = gain_sum(1)
    gain_start(2)
    line_sum(3)
    for turn in range(3):
        for sub in SUBS:
            unit_by = far_first(sub)[turn]
            rs_sum(1, sub, unit_by)
            go(last_copy(sub, unit_by % 4))
    for sub in SUBS:
        rs_sum(1, sub, 0)
    lax.fori_loop(13, 16, weight_tile, 0)
    gain_grad[...] = gain_sum(2)
    own[...] = f32(tokens[place[1], place[0], (place[2] % 2) * 2 + place[2] // 2])[8:]
    for sub in SUBS:
        _, _, lo, size = SCATTER[sub]
        for by in (1, 2, 3):
            last_copy(sub, by).wait_recv()
        columns = (slice(None), pl.ds(lo, size))
        summed = f32(got1[(2, place[SCATTER[sub][0][0]], *columns)])
        for by in (1, 2, 3):
            summed = summed + f32(got2[(by - 1, *columns)])
        total[:, pl.ds(lo, size)] = summed[:8]
        total[:, pl.ds(HALF + lo, size)] = summed[8:]
    for copy in started:
        copy.wait_send()


def finish(
    up_grad, down_grad, total, unit, inverse, own, gain_grad, gain,
    input_out, gain_out, up_out, down_out,
    input_rows, sem,
):
    PIECES = 4
    copies = [pltpu.make_async_copy(gain_grad, gain_out, sem.at[0])]
    for piece in range(PIECES):
        for which, (source, target) in enumerate(((up_grad, up_out), (down_grad, down_out))):
            size = source.shape[0] // PIECES
            at = pl.ds(piece * size, size)
            copies.append(pltpu.make_async_copy(source.at[at, :], target.at[at, :], sem.at[2 + 2 * piece + which]))
    for copy in copies:
        copy.start()

    scaled = total[...] * f32(gain[...])
    units = unit[...]
    inner_mean = jnp.mean(scaled, axis=-1, keepdims=True)
    proj_mean = jnp.mean(scaled * units, axis=-1, keepdims=True)
    change = inverse[:, 0:1] * (scaled - inner_mean - units * proj_mean)
    input_rows[...] = (own[...] + change).astype(jnp.bfloat16)
    copies.append(pltpu.make_async_copy(input_rows, input_out, sem.at[1]))
    copies[-1].start()
    for copy in copies:
        copy.wait()


def on_device(upstream, saved_input, norm_gain, up_weight, down_weight):
    bf16, f4 = jnp.bfloat16, jnp.float32
    vmem, hbm = pl.BlockSpec(memory_space=pltpu.VMEM), pl.BlockSpec(memory_space=pl.ANY)
    dma = pltpu.SemaphoreType.DMA
    held = pl.pallas_call(
        kernel,
        out_shape=[
            pltpu.VMEM((D, HID), f4),
            pltpu.VMEM((HID, D), f4),
            pltpu.VMEM((ROWS, D), f4),
            pltpu.VMEM((ROWS, D), f4),
            pltpu.VMEM((ROWS, 128), f4),
            pltpu.VMEM((ROWS, D), f4),
            pltpu.VMEM((1, D), f4),
        ],
        in_specs=[vmem, vmem, vmem, hbm, hbm],
        out_specs=[vmem] * 7,
        scratch_shapes=[
            pltpu.VMEM((4, 4, 4, 16, D), bf16),
            pltpu.VMEM((2, 4, 4, 2, 16, HID), bf16),
            pltpu.VMEM((D, HID), bf16),
            pltpu.VMEM((4, 4, 4, 16, HALF), bf16),
            pltpu.VMEM((3, 4, 4, 16, HALF), bf16),
            pltpu.VMEM((3, 4, 16, HALF), bf16),
            pltpu.VMEM((3, 16, HALF), bf16),
            pltpu.VMEM((4, 4, 4, 16, 2 * HID), f4),
            pltpu.VMEM((ROWS, D), f4),
            pltpu.VMEM((ROWS, D), f4),
            pltpu.VMEM((ROWS, D), f4),
            pltpu.VMEM((3, 4, 1, D), f4),
            dma((3,)), dma((2,)),
            dma((6, 9, 3)), dma((6, 9, 3)), dma((6, 9, 3)), dma((6, 9, 3)),
            dma((3, 3)), dma((3, 3)),
        ],
        compiler_params=pltpu.CompilerParams(
            collective_id=0, has_side_effects=True, vmem_limit_bytes=42 * 2**20
        ),
        name="section_backward",
    )(upstream[0], saved_input[0], norm_gain, up_weight[0], down_weight[0].reshape(4, 4, 16, D))
    held = [pltpu.with_memory_space_constraint(array, pltpu.VMEM) for array in held]
    input_grad, gain_grad, up_grad, down_grad = pl.pallas_call(
        finish,
        out_shape=[
            jax.ShapeDtypeStruct((ROWS, D), bf16),
            jax.ShapeDtypeStruct((1, D), f4),
            jax.ShapeDtypeStruct((D, HID), f4),
            jax.ShapeDtypeStruct((HID, D), f4),
        ],
        in_specs=[vmem] * 8,
        out_specs=[hbm] * 4,
        scratch_shapes=[
            pltpu.VMEM((ROWS, D), bf16),
            dma((10,)),
        ],
        compiler_params=pltpu.CompilerParams(vmem_limit_bytes=4 * 2**20),
        name="finish",
    )(*held, norm_gain)
    return (input_grad[None], up_grad[None], down_grad[None], gain_grad)


def solution(mesh):
    in_specs = (
        P("section", ("dp", "tensor"), None),
        P("section", ("dp", "tensor"), None),
        P("section", None),
        P("section", None, ("dp", "tensor")),
        P("section", ("dp", "tensor"), None),
    )
    out_specs = (
        P("section", ("dp", "tensor"), None),
        P("section", None, ("dp", "tensor")),
        P("section", ("dp", "tensor"), None),
        P("section", None),
    )
    return jax.shard_map(
        on_device, mesh=mesh, in_specs=in_specs, out_specs=out_specs, check_vma=False
    )
```

```python
import jax
import jax.numpy as jnp
from jax import lax
from jax.experimental import pallas as pl
from jax.experimental.pallas import tpu as pltpu
from jax.sharding import PartitionSpec as P

gelu_scale = 0.7978845608028654
cubic_coef = 0.044715

D = 8192
HALF = D // 2
HID = 256
ROWS = 8
MESH = pl.DeviceIdType.MESH

ORDERS = ((2, 1, 0), (0, 2, 1), (1, 0, 2))


def cut(pieces):
    return tuple(
        (ORDERS[number // 2], 1 if number % 2 == 0 else -1, at * 128, count * 128)
        for number, (at, count) in enumerate(pieces)
    )


GATHER = cut(((0, 11), (32, 11), (11, 11), (43, 10), (22, 10), (53, 11)))
SCATTER = cut(((0, 6), (6, 5), (11, 6), (17, 5), (22, 5), (27, 5)))
SUBS = range(6)
TURNS = (0, 2, 4, 1, 3, 5)


def gelu_pair(hidden):
    tanh_part = jnp.tanh(gelu_scale * (hidden + cubic_coef * hidden * hidden * hidden))
    gelu_out = 0.5 * hidden * (1.0 + tanh_part)
    derivative = 0.5 * (1.0 + tanh_part) + 0.5 * hidden * (
        1.0 - tanh_part * tanh_part
    ) * gelu_scale * (1.0 + 3.0 * cubic_coef * hidden * hidden)
    return (gelu_out, derivative)


def f32(value):
    return value.astype(jnp.float32)


def folded(rows):
    return jnp.concatenate([rows[:, :HALF], rows[:, HALF:]], axis=0)


def apart(blocks, size):
    wide = f32(blocks).reshape(-1, 16, size)
    return tuple(half.reshape(-1, size).astype(jnp.bfloat16) for half in (wide[:, :8], wide[:, 8:]))


def kernel(
    upstream, saved, gain, up_hbm, down_hbm,
    up_grad, down_grad, total, unit, inverse, own, gain_grad,
    tokens, weights, up, part, got0, got1, got2, hid, sent_rows, gain_acc, gain_slots,
    load_sem, swap_sem, ag_send, ag_recv, rs_send, rs_recv, gain_send, gain_recv,
):
    section = lax.axis_index("section")
    dp = lax.axis_index("dp")
    tensor = lax.axis_index("tensor")
    place = (dp // 2, tensor // 2, (tensor % 2) * 2 + dp % 2)
    started = []

    def go(copy):
        copy.start()
        started.append(copy)

    def device_at(z, y, x):
        return (section, z * 2 + x % 2, y * 2 + x // 2)

    def moved(axis, by):
        return lax.rem(place[axis] + (by + 4), 4)

    def neighbour(axis, by):
        there = list(place)
        there[axis] = moved(axis, by)
        return device_at(*there)

    partner = (1 - section, dp, tensor)

    barrier = pltpu.get_barrier_semaphore()
    others = [neighbour(axis, by) for axis in range(3) for by in (1, 2, 3)] + [partner]
    for other in others:
        pl.semaphore_signal(barrier, inc=1, device_id=other, device_id_type=MESH)
    sent_rows[...] = folded(f32(upstream[...])).astype(jnp.bfloat16)
    rows = f32(saved[...])
    centered = rows - jnp.mean(rows, axis=-1, keepdims=True)
    spread = lax.rsqrt(jnp.mean(centered * centered, axis=-1, keepdims=True) + 1e-05)
    inverse[...] = jnp.broadcast_to(spread, inverse.shape)
    unit[...] = centered * spread
    tokens[place[0], place[1], place[2], :, 0:HALF] = folded(unit[...] * f32(gain[...])).astype(jnp.bfloat16)
    pl.semaphore_wait(barrier, len(others))

    swap = pltpu.make_async_remote_copy(
        src_ref=sent_rows, dst_ref=tokens.at[place[0], place[1], place[2], :, pl.ds(HALF, HALF)],
        send_sem=swap_sem.at[0], recv_sem=swap_sem.at[1], device_id=partner, device_id_type=MESH,
    )
    go(swap)

    def gathered(phase, sub, unit_by, where):
        order, _, lo, size = GATHER[sub]
        index = [slice(None)] * 3
        for later in range(phase, 3):
            index[order[later]] = place[order[later]]
        if phase:
            index[order[phase - 1]] = moved(order[phase - 1], unit_by)
        index[order[phase]] = where
        return tokens.at[(*index, slice(None), pl.ds(lo, size))]

    def slot(phase, unit_by):
        return 0 if phase == 0 else 4 * phase - 3 + unit_by % 4

    def ag_copy(phase, sub, unit_by, message, where, by):
        block = gathered(phase, sub, unit_by, where)
        return pltpu.make_async_remote_copy(
            src_ref=block, dst_ref=block,
            send_sem=ag_send.at[sub, slot(phase, unit_by), message],
            recv_sem=ag_recv.at[sub, slot(phase, unit_by), message],
            device_id=neighbour(GATHER[sub][0][phase], by), device_id_type=MESH,
        )

    def ag_start(phase, sub, unit_by=0):
        axis, way = GATHER[sub][0][phase], GATHER[sub][1]
        go(ag_copy(phase, sub, unit_by, 0, place[axis], way))
        go(ag_copy(phase, sub, unit_by, 1, place[axis], -way))

    def ag_forward(phase, sub, unit_by=0):
        axis, way = GATHER[sub][0][phase], GATHER[sub][1]
        ag_copy(phase, sub, unit_by, 0, moved(axis, -way), way).wait_recv()
        go(ag_copy(phase, sub, unit_by, 2, moved(axis, -way), way))

    def ag_wait(phase, sub, message, unit_by=0):
        axis, way = GATHER[sub][0][phase], GATHER[sub][1]
        ag_copy(phase, sub, unit_by, message, moved(axis, way if message == 1 else 2), way).wait_recv()

    def plane(order, where):
        index = [slice(None)] * 3
        index[order[2]] = where
        return tuple(index)

    def first_products(sub, by, lines=None):
        order, _, lo, size = GATHER[sub]
        places = []
        for line in (None,) if lines is None else lines:
            at = list(plane(order, moved(order[2], by)))
            if line is not None:
                at[order[1]] = moved(order[1], line)
            places.append(tuple(at))
        blocks = [tokens[(*at, slice(None), pl.ds(lo, size))].reshape(-1, 16, size) for at in places]
        halves = apart(blocks[0] if len(blocks) == 1 else jnp.concatenate(blocks, axis=0), size)
        products = []
        for half, rows in enumerate(halves):
            if sub % 2 == 0:
                matrix, dims = up[pl.ds(half * HALF + lo, size), :], (((1,), (0,)), ((), ()))
            else:
                matrix = part[half, :, :, :, pl.ds(lo - HALF, size)].reshape(HID, size)
                dims = (((1,), (1,)), ((), ()))
            products.append(lax.dot_general(rows, matrix, dims, preferred_element_type=jnp.float32))
        summed = products[0] + products[1]
        count = summed.shape[0] // len(places)
        shape = ((4, 4) if lines is None else (4,)) + (8, HID)
        corner = (pl.ds(0, 8), pl.ds(0, HID)) if sub % 2 == 0 else (pl.ds(8, 8), pl.ds(HID, HID))
        for turn, at in enumerate(places):
            hid[(*at, *corner)] += summed[turn * count : (turn + 1) * count].reshape(shape)

    def way_of(sub):
        return GATHER[sub][1]

    for half in range(2):
        if half:
            swap.wait_recv()
        for sub in SUBS[half::2]:
            ag_start(0, sub)
        for sub in SUBS[half::2]:
            ag_start(1, sub, 0)
    load_up = pltpu.make_async_copy(up_hbm, up, load_sem.at[0])
    load_down = [
        pltpu.make_async_copy(down_hbm.at[:, :, :, pl.ds(half * HALF, HALF)], part.at[half], load_sem.at[1 + half])
        for half in range(2)
    ]
    load_up.start()
    for load in load_down:
        load.start()
    hid[...] = jnp.zeros_like(hid)
    for sub in TURNS:
        ag_forward(0, sub)
        ag_start(1, sub, -way_of(sub))
    for sub in TURNS:
        ag_wait(0, sub, 1)
        ag_start(1, sub, way_of(sub))
    for sub in TURNS:
        ag_forward(1, sub, 0)
    for sub in TURNS:
        ag_wait(0, sub, 2)
        ag_start(1, sub, 2)
        ag_start(2, sub, 0)
    for sub in TURNS:
        ag_forward(1, sub, -way_of(sub))
    for sub in TURNS:
        ag_forward(1, sub, way_of(sub))
    for sub in TURNS:
        ag_forward(1, sub, 2)
        ag_start(2, sub, -way_of(sub))
    for sub in TURNS:
        for unit_by in range(4):
            ag_wait(1, sub, 1, unit_by)
        ag_start(2, sub, way_of(sub))
    for sub in TURNS:
        for unit_by in range(4):
            ag_wait(1, sub, 2, unit_by)
        ag_start(2, sub, 2)
    load_up.wait()
    for load in load_down:
        load.wait()
    for sub in TURNS:
        ag_forward(2, sub, 0)
    for sub in TURNS:
        first_products(sub, 0)
    for sub in TURNS:
        ag_forward(2, sub, -way_of(sub))
    for sub in TURNS:
        ag_forward(2, sub, way_of(sub))
    for sub in TURNS:
        ag_forward(2, sub, 2)
    for sub in TURNS:
        first_products(sub, -way_of(sub))
    for sub in TURNS:
        for unit_by in range(4):
            ag_wait(2, sub, 1, unit_by)
        first_products(sub, way_of(sub))
    for unit_by in (0, 1, 3):
        for sub in TURNS:
            ag_wait(2, sub, 2, unit_by)
    for sub in TURNS:
        first_products(sub, 2, (0, 1, -1))
    for sub in TURNS:
        ag_wait(2, sub, 2, 2)
        first_products(sub, 2, (2,))

    SWAPPED = (0, 2, 1, 3)

    def activate(step, carry):
        z, y = step // 4, step % 4
        act, derivative = gelu_pair(hid[z, y, :, 0:8, 0:HID])
        for x in range(4):
            hid[z, y, x, 0:8, HID:] = hid[y, z, SWAPPED[x], 8:16, HID:] * derivative[x]
            hid[z, y, x, 0:8, 0:HID] = act[x]
        return carry

    lax.fori_loop(0, 16, activate, 0)

    def lay_out(step, carry):
        z, y = step // 4, step % 4
        for pair in range(2):
            first, second = 2 * pair, 2 * pair + 1
            weights[0, z, y, pair] = jnp.concatenate(
                [hid[z, y, x, 0:8, HID:] for x in (first, second)], axis=0
            ).astype(jnp.bfloat16)
            weights[1, z, y, pair] = jnp.concatenate(
                [hid[y, z, SWAPPED[x], 0:8, 0:HID] for x in (first, second)], axis=0
            ).astype(jnp.bfloat16)
        return carry

    def second_products(sub, by):
        order, _, lo, size = SCATTER[sub]
        at = plane(order, moved(order[2], by))
        left = hid[(*at, pl.ds(0, 8), pl.ds(HID, HID))].reshape(128, HID).astype(jnp.bfloat16)
        halves = []
        for start in (lo, HALF + lo):
            halves.append(
                lax.dot_general(
                    left, up[pl.ds(start, size), :], (((1,), (1,)), ((), ())), preferred_element_type=jnp.float32
                ).reshape(4, 4, 8, size)
            )
        part[(*at, slice(None), pl.ds(lo, size))] = jnp.concatenate(halves, axis=2).astype(jnp.bfloat16)

    def two_axes(order, b_index, a_index=slice(None)):
        return tuple(b_index if axis == order[1] else a_index for axis in range(3) if axis != order[2])

    def landing(phase, sub, unit_by, message):
        order, _, lo, size = SCATTER[sub]
        columns = (slice(None), pl.ds(lo, size))
        if phase == 0:
            return got0.at[(message, *two_axes(order, moved(order[1], unit_by)), *columns)]
        return got1.at[(message, moved(order[0], unit_by), *columns)]

    def share(phase, sub, unit_by, by):
        order, _, lo, size = SCATTER[sub]
        columns = (slice(None), pl.ds(lo, size))
        where = moved(order[2 - phase], by)
        if phase == 0:
            index = list(plane(order, where))
            index[order[1]] = moved(order[1], unit_by)
            return part.at[(*index, *columns)]
        return got0.at[(2, *two_axes(order, where, moved(order[0], unit_by)), *columns)]

    def rs_copy(phase, sub, unit_by, message):
        order, way = SCATTER[sub][0], SCATTER[sub][1]
        if message == 0:
            source, by = share(phase, sub, unit_by, 2), -way
        elif message == 1:
            source, by = share(phase, sub, unit_by, way), way
        else:
            source, by = landing(phase, sub, unit_by, 0), -way
        at = slot(2 - phase, unit_by)
        return pltpu.make_async_remote_copy(
            src_ref=source, dst_ref=landing(phase, sub, unit_by, message),
            send_sem=rs_send.at[sub, at, message], recv_sem=rs_recv.at[sub, at, message],
            device_id=neighbour(order[2 - phase], by), device_id_type=MESH,
        )

    def rs_start(phase, sub, unit_by, message):
        go(rs_copy(phase, sub, unit_by, message))

    def rs_forward(phase, sub, unit_by=0):
        rs_copy(phase, sub, unit_by, 0).wait_recv()
        ref = landing(phase, sub, unit_by, 0)
        mine = share(phase, sub, unit_by, -way_of(sub))
        ref[...] = (f32(ref[...]) + f32(mine[...])).astype(jnp.bfloat16)
        rs_start(phase, sub, unit_by, 2)

    def rs_sum(phase, sub, unit_by=0):
        rs_copy(phase, sub, unit_by, 1).wait_recv()
        rs_copy(phase, sub, unit_by, 2).wait_recv()
        mine = share(phase, sub, unit_by, 0)
        ref = landing(phase, sub, unit_by, 2)
        summed = f32(mine[...]) + f32(landing(phase, sub, unit_by, 1)[...]) + f32(ref[...])
        ref[...] = summed.astype(jnp.bfloat16)

    def last_copy(sub, by):
        order, _, lo, size = SCATTER[sub]
        columns = (slice(None), pl.ds(lo, size))
        return pltpu.make_async_remote_copy(
            src_ref=got1.at[(2, moved(order[0], by), *columns)], dst_ref=got2.at[(by - 1, *columns)],
            send_sem=rs_send.at[sub, 0, by - 1], recv_sem=rs_recv.at[sub, 0, by - 1],
            device_id=neighbour(order[0], by), device_id_type=MESH,
        )

    def far_first(sub):
        return (2, way_of(sub), -way_of(sub), 0)

    for sub in SUBS:
        second_products(sub, 2)
        for turn in (0, 1):
            rs_start(0, sub, far_first(sub)[turn], 0)
    for sub in SUBS:
        second_products(sub, way_of(sub))
        for turn in (0, 1):
            rs_start(0, sub, far_first(sub)[turn], 1)
    for sub in SUBS:
        second_products(sub, -way_of(sub))

    def line_step(turn):
        for sub in SUBS:
            rs_forward(0, sub, far_first(sub)[turn])
            if turn < 2:
                rs_start(0, sub, far_first(sub)[turn + 2], 0)
            if 0 < turn < 3:
                rs_start(0, sub, far_first(sub)[turn + 1], 1)

    def line_sum(turn):
        for sub in SUBS:
            rs_sum(0, sub, far_first(sub)[turn])
            if turn < 2:
                for unit_by in far_first(sub):
                    rs_start(1, sub, unit_by, turn)

    line_step(0)
    lax.fori_loop(0, 16, lay_out, 0)
    line_step(1)
    for sub in SUBS:
        second_products(sub, 0)
    line_sum(0)
    line_step(2)

    def gain_tile(step, carry):
        at = pl.ds(pl.multiple_of(step * 256, 256), 256)
        also = pl.ds(pl.multiple_of(HALF + step * 256, 256), 256)
        sums = jnp.zeros((16, 256), jnp.float32)
        for z in range(4):
            sums = sums + jnp.sum((f32(part[z, :, :, :, at]) * f32(tokens[z, :, :, :, at])).reshape(16, 16, 256), axis=0)
        gain_acc[:, at] = sums[:8]
        gain_acc[:, also] = sums[8:]
        return carry

    lax.fori_loop(0, HALF // 256, gain_tile, 0)
    gain_slots[0, place[2]] = jnp.sum(gain_acc[...], axis=0, keepdims=True) / f32(gain[...])

    def gain_copy(phase, by, owner):
        axis = 2 - phase
        return pltpu.make_async_remote_copy(
            src_ref=gain_slots.at[phase, owner], dst_ref=gain_slots.at[phase, owner],
            send_sem=gain_send.at[phase, by - 1], recv_sem=gain_recv.at[phase, by - 1],
            device_id=neighbour(axis, by), device_id_type=MESH,
        )

    def gain_start(phase):
        for by in (1, 2, 3):
            go(gain_copy(phase, by, place[2 - phase]))

    def gain_sum(phase):
        for by in (1, 2, 3):
            gain_copy(phase, by, moved(2 - phase, -by)).wait_recv()
        return (gain_slots[phase, 0] + gain_slots[phase, 1]) + (gain_slots[phase, 2] + gain_slots[phase, 3])

    TILE = 256

    def weight_tile(step, carry):
        normed_at = pl.ds(pl.multiple_of(step * TILE, TILE), TILE)
        grad_at = pl.ds(pl.multiple_of(HALF + step * TILE, TILE), TILE)
        for half, rows in enumerate(apart(tokens[:, :, :, :, normed_at], TILE)):
            up_grad[pl.ds(pl.multiple_of(half * HALF + step * TILE, TILE), TILE), :] = lax.dot_general(
                rows, weights[0].reshape(512, HID), (((0,), (0,)), ((), ())), preferred_element_type=jnp.float32
            )
        for half, rows in enumerate(apart(tokens[:, :, :, :, grad_at], TILE)):
            down_grad[:, pl.ds(pl.multiple_of(half * HALF + step * TILE, TILE), TILE)] = lax.dot_general(
                weights[1].reshape(512, HID), rows, (((0,), (0,)), ((), ())), preferred_element_type=jnp.float32
            )
        return carry

    gain_start(0)
    line_sum(1)
    line_step(3)
    lax.fori_loop(0, 6, weight_tile, 0)
    gain_slots[1, place[1]] = gain_sum(0)
    gain_start(1)
    line_sum(2)
    for turn in range(4):
        for sub in SUBS:
            rs_forward(1, sub, far_first(sub)[turn])
    lax.fori_loop(6, 13, weight_tile, 0)
    gain_slots[2, place[0]] = gain_sum(1)
    gain_start(2)
    line_sum(3)
    for turn in range(3):
        for sub in SUBS:
            unit_by = far_first(sub)[turn]
            rs_sum(1, sub, unit_by)
            go(last_copy(sub, unit_by % 4))
    for sub in SUBS:
        rs_sum(1, sub, 0)
    lax.fori_loop(13, 16, weight_tile, 0)
    gain_grad[...] = gain_sum(2)
    kept = f32(tokens[place[1], place[0], (place[2] % 2) * 2 + place[2] // 2, :, HALF:])
    own[:, :HALF] = kept[:8]
    own[:, HALF:] = kept[8:]
    for sub in SUBS:
        _, _, lo, size = SCATTER[sub]
        for by in (1, 2, 3):
            last_copy(sub, by).wait_recv()
        columns = (slice(None), pl.ds(lo, size))
        summed = f32(got1[(2, place[SCATTER[sub][0][0]], *columns)])
        for by in (1, 2, 3):
            summed = summed + f32(got2[(by - 1, *columns)])
        total[:, pl.ds(lo, size)] = summed[:8]
        total[:, pl.ds(HALF + lo, size)] = summed[8:]
    for copy in started:
        copy.wait_send()


def finish(
    up_grad, down_grad, total, unit, inverse, own, gain_grad, gain,
    input_out, gain_out, up_out, down_out,
    input_rows, sem,
):
    PIECES = 4
    copies = [pltpu.make_async_copy(gain_grad, gain_out, sem.at[0])]
    for piece in range(PIECES):
        for which, (source, target) in enumerate(((up_grad, up_out), (down_grad, down_out))):
            size = source.shape[0] // PIECES
            at = pl.ds(piece * size, size)
            copies.append(pltpu.make_async_copy(source.at[at, :], target.at[at, :], sem.at[2 + 2 * piece + which]))
    for copy in copies:
        copy.start()

    scaled = total[...] * f32(gain[...])
    units = unit[...]
    inner_mean = jnp.mean(scaled, axis=-1, keepdims=True)
    proj_mean = jnp.mean(scaled * units, axis=-1, keepdims=True)
    change = inverse[:, 0:1] * (scaled - inner_mean - units * proj_mean)
    input_rows[...] = (own[...] + change).astype(jnp.bfloat16)
    copies.append(pltpu.make_async_copy(input_rows, input_out, sem.at[1]))
    copies[-1].start()
    for copy in copies:
        copy.wait()


def on_device(upstream, saved_input, norm_gain, up_weight, down_weight):
    bf16, f4 = jnp.bfloat16, jnp.float32
    vmem, hbm = pl.BlockSpec(memory_space=pltpu.VMEM), pl.BlockSpec(memory_space=pl.ANY)
    dma = pltpu.SemaphoreType.DMA
    held = pl.pallas_call(
        kernel,
        out_shape=[
            pltpu.VMEM((D, HID), f4),
            pltpu.VMEM((HID, D), f4),
            pltpu.VMEM((ROWS, D), f4),
            pltpu.VMEM((ROWS, D), f4),
            pltpu.VMEM((ROWS, 128), f4),
            pltpu.VMEM((ROWS, D), f4),
            pltpu.VMEM((1, D), f4),
        ],
        in_specs=[vmem, vmem, vmem, hbm, hbm],
        out_specs=[vmem] * 7,
        scratch_shapes=[
            pltpu.VMEM((4, 4, 4, 16, D), bf16),
            pltpu.VMEM((2, 4, 4, 2, 16, HID), bf16),
            pltpu.VMEM((D, HID), bf16),
            pltpu.VMEM((4, 4, 4, 16, HALF), bf16),
            pltpu.VMEM((3, 4, 4, 16, HALF), bf16),
            pltpu.VMEM((3, 4, 16, HALF), bf16),
            pltpu.VMEM((3, 16, HALF), bf16),
            pltpu.VMEM((4, 4, 4, 16, 2 * HID), f4),
            pltpu.VMEM((16, HALF), bf16),
            pltpu.VMEM((ROWS, D), f4),
            pltpu.VMEM((3, 4, 1, D), f4),
            dma((3,)), dma((2,)),
            dma((6, 9, 3)), dma((6, 9, 3)), dma((6, 9, 3)), dma((6, 9, 3)),
            dma((3, 3)), dma((3, 3)),
        ],
        compiler_params=pltpu.CompilerParams(
            collective_id=0, has_side_effects=True, vmem_limit_bytes=42 * 2**20
        ),
        name="section_backward",
    )(upstream[0], saved_input[0], norm_gain, up_weight[0], down_weight[0].reshape(4, 4, 16, D))
    held = [pltpu.with_memory_space_constraint(array, pltpu.VMEM) for array in held]
    input_grad, gain_grad, up_grad, down_grad = pl.pallas_call(
        finish,
        out_shape=[
            jax.ShapeDtypeStruct((ROWS, D), bf16),
            jax.ShapeDtypeStruct((1, D), f4),
            jax.ShapeDtypeStruct((D, HID), f4),
            jax.ShapeDtypeStruct((HID, D), f4),
        ],
        in_specs=[vmem] * 8,
        out_specs=[hbm] * 4,
        scratch_shapes=[
            pltpu.VMEM((ROWS, D), bf16),
            dma((10,)),
        ],
        compiler_params=pltpu.CompilerParams(vmem_limit_bytes=4 * 2**20),
        name="finish",
    )(*held, norm_gain)
    return (input_grad[None], up_grad[None], down_grad[None], gain_grad)


def solution(mesh):
    in_specs = (
        P("section", ("dp", "tensor"), None),
        P("section", ("dp", "tensor"), None),
        P("section", None),
        P("section", None, ("dp", "tensor")),
        P("section", ("dp", "tensor"), None),
    )
    out_specs = (
        P("section", ("dp", "tensor"), None),
        P("section", None, ("dp", "tensor")),
        P("section", ("dp", "tensor"), None),
        P("section", None),
    )
    return jax.shard_map(
        on_device, mesh=mesh, in_specs=in_specs, out_specs=out_specs, check_vma=False
    )
```

```python
import jax
import jax.numpy as jnp
from jax import lax
from jax.experimental import pallas as pl
from jax.experimental.pallas import tpu as pltpu
from jax.sharding import PartitionSpec as P

gelu_scale = 0.7978845608028654
cubic_coef = 0.044715

D = 8192
HALF = D // 2
HID = 256
ROWS = 8
MESH = pl.DeviceIdType.MESH

ORDERS = ((2, 1, 0), (0, 2, 1), (1, 0, 2))


def cut(pieces):
    return tuple(
        (ORDERS[number // 2], 1 if number % 2 == 0 else -1, at * 128, count * 128)
        for number, (at, count) in enumerate(pieces)
    )


GATHER = cut(((0, 11), (32, 11), (11, 11), (43, 10), (22, 10), (53, 11)))
SCATTER = cut(((0, 6), (6, 5), (11, 6), (17, 5), (22, 5), (27, 5)))
SUBS = range(6)
TURNS = (0, 2, 4, 1, 3, 5)


def gelu_pair(hidden):
    tanh_part = jnp.tanh(gelu_scale * (hidden + cubic_coef * hidden * hidden * hidden))
    gelu_out = 0.5 * hidden * (1.0 + tanh_part)
    derivative = 0.5 * (1.0 + tanh_part) + 0.5 * hidden * (
        1.0 - tanh_part * tanh_part
    ) * gelu_scale * (1.0 + 3.0 * cubic_coef * hidden * hidden)
    return (gelu_out, derivative)


def f32(value):
    return value.astype(jnp.float32)


def folded(rows):
    return jnp.concatenate([rows[:, :HALF], rows[:, HALF:]], axis=0)


def apart(blocks, size):
    wide = f32(blocks).reshape(-1, 16, size)
    return tuple(half.reshape(-1, size).astype(jnp.bfloat16) for half in (wide[:, :8], wide[:, 8:]))


def kernel(
    upstream, saved, gain, up_hbm, down_hbm,
    up_grad, down_grad, total, unit, inverse, own, gain_grad,
    tokens, weights, up, part, got0, got1, got2, hid, sent_rows, gain_acc, gain_slots,
    load_sem, swap_sem, ag_send, ag_recv, rs_send, rs_recv, gain_send, gain_recv,
):
    section = lax.axis_index("section")
    dp = lax.axis_index("dp")
    tensor = lax.axis_index("tensor")
    place = (dp // 2, tensor // 2, (tensor % 2) * 2 + dp % 2)
    started = []

    def go(copy):
        copy.start()
        started.append(copy)

    def settle(count):
        for copy in started[:count]:
            copy.wait_send()
        del started[:count]

    def device_at(z, y, x):
        return (section, z * 2 + x % 2, y * 2 + x // 2)

    def moved(axis, by):
        return lax.rem(place[axis] + (by + 4), 4)

    def neighbour(axis, by):
        there = list(place)
        there[axis] = moved(axis, by)
        return device_at(*there)

    partner = (1 - section, dp, tensor)

    barrier = pltpu.get_barrier_semaphore()
    others = [neighbour(axis, by) for axis in range(3) for by in (1, 2, 3)] + [partner]
    for other in others:
        pl.semaphore_signal(barrier, inc=1, device_id=other, device_id_type=MESH)
    sent_rows[...] = folded(f32(upstream[...])).astype(jnp.bfloat16)
    rows = f32(saved[...])
    centered = rows - jnp.mean(rows, axis=-1, keepdims=True)
    spread = lax.rsqrt(jnp.mean(centered * centered, axis=-1, keepdims=True) + 1e-05)
    inverse[...] = jnp.broadcast_to(spread, inverse.shape)
    unit[...] = centered * spread
    tokens[place[0], place[1], place[2], :, 0:HALF] = folded(unit[...] * f32(gain[...])).astype(jnp.bfloat16)
    pl.semaphore_wait(barrier, len(others))

    swap = pltpu.make_async_remote_copy(
        src_ref=sent_rows, dst_ref=tokens.at[place[0], place[1], place[2], :, pl.ds(HALF, HALF)],
        send_sem=swap_sem.at[0], recv_sem=swap_sem.at[1], device_id=partner, device_id_type=MESH,
    )
    go(swap)

    def gathered(phase, sub, unit_by, where):
        order, _, lo, size = GATHER[sub]
        index = [slice(None)] * 3
        for later in range(phase, 3):
            index[order[later]] = place[order[later]]
        if phase:
            index[order[phase - 1]] = moved(order[phase - 1], unit_by)
        index[order[phase]] = where
        return tokens.at[(*index, slice(None), pl.ds(lo, size))]

    def slot(phase, unit_by):
        return 0 if phase == 0 else 4 * phase - 3 + unit_by % 4

    def ag_copy(phase, sub, unit_by, message, where, by):
        block = gathered(phase, sub, unit_by, where)
        return pltpu.make_async_remote_copy(
            src_ref=block, dst_ref=block,
            send_sem=ag_send.at[sub, slot(phase, unit_by), message],
            recv_sem=ag_recv.at[sub, slot(phase, unit_by), message],
            device_id=neighbour(GATHER[sub][0][phase], by), device_id_type=MESH,
        )

    def ag_start(phase, sub, unit_by=0):
        axis, way = GATHER[sub][0][phase], GATHER[sub][1]
        go(ag_copy(phase, sub, unit_by, 0, place[axis], way))
        go(ag_copy(phase, sub, unit_by, 1, place[axis], -way))

    def ag_forward(phase, sub, unit_by=0):
        axis, way = GATHER[sub][0][phase], GATHER[sub][1]
        ag_copy(phase, sub, unit_by, 0, moved(axis, -way), way).wait_recv()
        go(ag_copy(phase, sub, unit_by, 2, moved(axis, -way), way))

    def ag_wait(phase, sub, message, unit_by=0):
        axis, way = GATHER[sub][0][phase], GATHER[sub][1]
        ag_copy(phase, sub, unit_by, message, moved(axis, way if message == 1 else 2), way).wait_recv()

    def plane(order, where):
        index = [slice(None)] * 3
        index[order[2]] = where
        return tuple(index)

    def first_products(sub, by, lines=None):
        order, _, lo, size = GATHER[sub]
        places = []
        for line in (None,) if lines is None else lines:
            at = list(plane(order, moved(order[2], by)))
            if line is not None:
                at[order[1]] = moved(order[1], line)
            places.append(tuple(at))
        blocks = [tokens[(*at, slice(None), pl.ds(lo, size))].reshape(-1, 16, size) for at in places]
        halves = apart(blocks[0] if len(blocks) == 1 else jnp.concatenate(blocks, axis=0), size)
        products = []
        for half, rows in enumerate(halves):
            if sub % 2 == 0:
                matrix, dims = up[pl.ds(half * HALF + lo, size), :], (((1,), (0,)), ((), ()))
            else:
                matrix = part[half, :, :, :, pl.ds(lo - HALF, size)].reshape(HID, size)
                dims = (((1,), (1,)), ((), ()))
            products.append(lax.dot_general(rows, matrix, dims, preferred_element_type=jnp.float32))
        summed = products[0] + products[1]
        count = summed.shape[0] // len(places)
        shape = ((4, 4) if lines is None else (4,)) + (8, HID)
        corner = (pl.ds(0, 8), pl.ds(0, HID)) if sub % 2 == 0 else (pl.ds(8, 8), pl.ds(HID, HID))
        for turn, at in enumerate(places):
            hid[(*at, *corner)] += summed[turn * count : (turn + 1) * count].reshape(shape)

    def way_of(sub):
        return GATHER[sub][1]

    for half in range(2):
        if half:
            swap.wait_recv()
        for sub in SUBS[half::2]:
            ag_start(0, sub)
        for sub in SUBS[half::2]:
            ag_start(1, sub, 0)
    load_up = pltpu.make_async_copy(up_hbm, up, load_sem.at[0])
    load_down = [
        pltpu.make_async_copy(down_hbm.at[:, :, :, pl.ds(half * HALF, HALF)], part.at[half], load_sem.at[1 + half])
        for half in range(2)
    ]
    load_up.start()
    for load in load_down:
        load.start()
    hid[...] = jnp.zeros_like(hid)
    for sub in TURNS:
        ag_forward(0, sub)
        ag_start(1, sub, -way_of(sub))
    for sub in TURNS:
        ag_wait(0, sub, 1)
        ag_start(1, sub, way_of(sub))
    for sub in TURNS:
        ag_forward(1, sub, 0)
    for sub in TURNS:
        ag_wait(0, sub, 2)
        ag_start(1, sub, 2)
        ag_start(2, sub, 0)
    for sub in TURNS:
        ag_forward(1, sub, -way_of(sub))
    for sub in TURNS:
        ag_forward(1, sub, way_of(sub))
    for sub in TURNS:
        ag_forward(1, sub, 2)
        ag_start(2, sub, -way_of(sub))
    for sub in TURNS:
        for unit_by in range(4):
            ag_wait(1, sub, 1, unit_by)
        ag_start(2, sub, way_of(sub))
    for sub in TURNS:
        for unit_by in range(4):
            ag_wait(1, sub, 2, unit_by)
        ag_start(2, sub, 2)
    load_up.wait()
    for load in load_down:
        load.wait()
    for sub in TURNS:
        ag_forward(2, sub, 0)
    for sub in TURNS:
        first_products(sub, 0)
    for sub in TURNS:
        ag_forward(2, sub, -way_of(sub))
    for sub in TURNS:
        ag_forward(2, sub, way_of(sub))
    for sub in TURNS:
        ag_forward(2, sub, 2)
    for sub in TURNS:
        first_products(sub, -way_of(sub))
    for sub in TURNS:
        for unit_by in range(4):
            ag_wait(2, sub, 1, unit_by)
        first_products(sub, way_of(sub))
    for unit_by in (0, 1, 3):
        for sub in TURNS:
            ag_wait(2, sub, 2, unit_by)
    for sub in TURNS:
        first_products(sub, 2, (0, 1, -1))
    for sub in TURNS:
        ag_wait(2, sub, 2, 2)
        first_products(sub, 2, (2,))

    SWAPPED = (0, 2, 1, 3)

    def activate(z, carry):
        for y in range(4):
            act, derivative = gelu_pair(hid[z, y, :, 0:8, 0:HID])
            for x in range(4):
                hid[z, y, x, 0:8, HID:] = hid[y, z, SWAPPED[x], 8:16, HID:] * derivative[x]
                hid[z, y, x, 0:8, 0:HID] = act[x]
        return carry

    lax.fori_loop(0, 4, activate, 0)
    gathers = len(started)

    def lay_out(step, carry):
        z, y = step // 4, step % 4
        for pair in range(2):
            first, second = 2 * pair, 2 * pair + 1
            weights[0, z, y, pair] = jnp.concatenate(
                [hid[z, y, x, 0:8, HID:] for x in (first, second)], axis=0
            ).astype(jnp.bfloat16)
            weights[1, z, y, pair] = jnp.concatenate(
                [hid[y, z, SWAPPED[x], 0:8, 0:HID] for x in (first, second)], axis=0
            ).astype(jnp.bfloat16)
        return carry

    def second_products(sub, by):
        order, _, lo, size = SCATTER[sub]
        at = plane(order, moved(order[2], by))
        left = hid[(*at, pl.ds(0, 8), pl.ds(HID, HID))].reshape(128, HID).astype(jnp.bfloat16)
        halves = []
        for start in (lo, HALF + lo):
            halves.append(
                lax.dot_general(
                    left, up[pl.ds(start, size), :], (((1,), (1,)), ((), ())), preferred_element_type=jnp.float32
                ).reshape(4, 4, 8, size)
            )
        part[(*at, slice(None), pl.ds(lo, size))] = jnp.concatenate(halves, axis=2).astype(jnp.bfloat16)

    def two_axes(order, b_index, a_index=slice(None)):
        return tuple(b_index if axis == order[1] else a_index for axis in range(3) if axis != order[2])

    def landing(phase, sub, unit_by, message):
        order, _, lo, size = SCATTER[sub]
        columns = (slice(None), pl.ds(lo, size))
        if phase == 0:
            return got0.at[(message, *two_axes(order, moved(order[1], unit_by)), *columns)]
        return got1.at[(message, moved(order[0], unit_by), *columns)]

    def share(phase, sub, unit_by, by):
        order, _, lo, size = SCATTER[sub]
        columns = (slice(None), pl.ds(lo, size))
        where = moved(order[2 - phase], by)
        if phase == 0:
            index = list(plane(order, where))
            index[order[1]] = moved(order[1], unit_by)
            return part.at[(*index, *columns)]
        return got0.at[(2, *two_axes(order, where, moved(order[0], unit_by)), *columns)]

    def rs_copy(phase, sub, unit_by, message):
        order, way = SCATTER[sub][0], SCATTER[sub][1]
        if message == 0:
            source, by = share(phase, sub, unit_by, 2), -way
        elif message == 1:
            source, by = share(phase, sub, unit_by, way), way
        else:
            source, by = landing(phase, sub, unit_by, 0), -way
        at = slot(2 - phase, unit_by)
        return pltpu.make_async_remote_copy(
            src_ref=source, dst_ref=landing(phase, sub, unit_by, message),
            send_sem=rs_send.at[sub, at, message], recv_sem=rs_recv.at[sub, at, message],
            device_id=neighbour(order[2 - phase], by), device_id_type=MESH,
        )

    def rs_start(phase, sub, unit_by, message):
        go(rs_copy(phase, sub, unit_by, message))

    def rs_forward(phase, sub, unit_by=0):
        rs_copy(phase, sub, unit_by, 0).wait_recv()
        ref = landing(phase, sub, unit_by, 0)
        mine = share(phase, sub, unit_by, -way_of(sub))
        ref[...] = (f32(ref[...]) + f32(mine[...])).astype(jnp.bfloat16)
        rs_start(phase, sub, unit_by, 2)

    def rs_sum(phase, sub, unit_by=0):
        rs_copy(phase, sub, unit_by, 1).wait_recv()
        rs_copy(phase, sub, unit_by, 2).wait_recv()
        mine = share(phase, sub, unit_by, 0)
        ref = landing(phase, sub, unit_by, 2)
        summed = f32(mine[...]) + f32(landing(phase, sub, unit_by, 1)[...]) + f32(ref[...])
        ref[...] = summed.astype(jnp.bfloat16)

    def last_copy(sub, by):
        order, _, lo, size = SCATTER[sub]
        columns = (slice(None), pl.ds(lo, size))
        return pltpu.make_async_remote_copy(
            src_ref=got1.at[(2, moved(order[0], by), *columns)], dst_ref=got2.at[(by - 1, *columns)],
            send_sem=rs_send.at[sub, 0, by - 1], recv_sem=rs_recv.at[sub, 0, by - 1],
            device_id=neighbour(order[0], by), device_id_type=MESH,
        )

    def far_first(sub):
        return (2, way_of(sub), -way_of(sub), 0)

    for sub in SUBS:
        second_products(sub, 2)
        for turn in (0, 1):
            rs_start(0, sub, far_first(sub)[turn], 0)
    for sub in SUBS:
        second_products(sub, way_of(sub))
        for turn in (0, 1):
            rs_start(0, sub, far_first(sub)[turn], 1)
    for sub in SUBS:
        second_products(sub, -way_of(sub))

    def line_step(turn):
        for sub in SUBS:
            rs_forward(0, sub, far_first(sub)[turn])
            if turn < 2:
                rs_start(0, sub, far_first(sub)[turn + 2], 0)
            if 0 < turn < 3:
                rs_start(0, sub, far_first(sub)[turn + 1], 1)

    def line_sum(turn):
        for sub in SUBS:
            rs_sum(0, sub, far_first(sub)[turn])
            if turn < 2:
                for unit_by in far_first(sub):
                    rs_start(1, sub, unit_by, turn)

    line_step(0)
    lax.fori_loop(0, 16, lay_out, 0)
    settle(gathers)
    line_step(1)
    early = len(started)
    for sub in SUBS:
        second_products(sub, 0)
    line_sum(0)
    line_step(2)

    def gain_tile(step, carry):
        at = pl.ds(pl.multiple_of(step * 256, 256), 256)
        also = pl.ds(pl.multiple_of(HALF + step * 256, 256), 256)
        sums = jnp.zeros((16, 256), jnp.float32)
        for z in range(4):
            sums = sums + jnp.sum((f32(part[z, :, :, :, at]) * f32(tokens[z, :, :, :, at])).reshape(16, 16, 256), axis=0)
        gain_acc[:, at] = sums[:8]
        gain_acc[:, also] = sums[8:]
        return carry

    lax.fori_loop(0, HALF // 256, gain_tile, 0)
    gain_slots[0, place[2]] = jnp.sum(gain_acc[...], axis=0, keepdims=True) / f32(gain[...])

    def gain_copy(phase, by, owner):
        axis = 2 - phase
        return pltpu.make_async_remote_copy(
            src_ref=gain_slots.at[phase, owner], dst_ref=gain_slots.at[phase, owner],
            send_sem=gain_send.at[phase, by - 1], recv_sem=gain_recv.at[phase, by - 1],
            device_id=neighbour(axis, by), device_id_type=MESH,
        )

    def gain_start(phase):
        for by in (1, 2, 3):
            go(gain_copy(phase, by, place[2 - phase]))

    def gain_sum(phase):
        for by in (1, 2, 3):
            gain_copy(phase, by, moved(2 - phase, -by)).wait_recv()
        return (gain_slots[phase, 0] + gain_slots[phase, 1]) + (gain_slots[phase, 2] + gain_slots[phase, 3])

    TILE = 256

    def weight_tile(step, carry):
        normed_at = pl.ds(pl.multiple_of(step * TILE, TILE), TILE)
        grad_at = pl.ds(pl.multiple_of(HALF + step * TILE, TILE), TILE)
        for half, rows in enumerate(apart(tokens[:, :, :, :, normed_at], TILE)):
            up_grad[pl.ds(pl.multiple_of(half * HALF + step * TILE, TILE), TILE), :] = lax.dot_general(
                rows, weights[0].reshape(512, HID), (((0,), (0,)), ((), ())), preferred_element_type=jnp.float32
            )
        for half, rows in enumerate(apart(tokens[:, :, :, :, grad_at], TILE)):
            down_grad[:, pl.ds(pl.multiple_of(half * HALF + step * TILE, TILE), TILE)] = lax.dot_general(
                weights[1].reshape(512, HID), rows, (((0,), (0,)), ((), ())), preferred_element_type=jnp.float32
            )
        return carry

    gain_start(0)
    line_sum(1)
    line_step(3)
    late = len(started) - early
    lax.fori_loop(0, 8, weight_tile, 0)
    settle(early)
    gain_slots[1, place[1]] = gain_sum(0)
    gain_start(1)
    line_sum(2)
    for turn in range(4):
        for sub in SUBS:
            rs_forward(1, sub, far_first(sub)[turn])
    second = len(started) - late
    lax.fori_loop(8, 16, weight_tile, 0)
    settle(late)
    gain_slots[2, place[0]] = gain_sum(1)
    gain_start(2)
    line_sum(3)
    for turn in range(3):
        for sub in SUBS:
            unit_by = far_first(sub)[turn]
            rs_sum(1, sub, unit_by)
            go(last_copy(sub, unit_by % 4))
    for sub in SUBS:
        rs_sum(1, sub, 0)
    settle(second)
    gain_grad[...] = gain_sum(2)
    kept = f32(tokens[place[1], place[0], (place[2] % 2) * 2 + place[2] // 2, :, HALF:])
    own[:, :HALF] = kept[:8]
    own[:, HALF:] = kept[8:]
    for sub in SUBS:
        _, _, lo, size = SCATTER[sub]
        for by in (1, 2, 3):
            last_copy(sub, by).wait_recv()
        columns = (slice(None), pl.ds(lo, size))
        summed = f32(got1[(2, place[SCATTER[sub][0][0]], *columns)])
        for by in (1, 2, 3):
            summed = summed + f32(got2[(by - 1, *columns)])
        total[:, pl.ds(lo, size)] = summed[:8]
        total[:, pl.ds(HALF + lo, size)] = summed[8:]
    settle(len(started))


def finish(
    up_grad, down_grad, total, unit, inverse, own, gain_grad, gain,
    input_out, gain_out, up_out, down_out,
    input_rows, sem,
):
    PIECES = 4
    copies = [pltpu.make_async_copy(gain_grad, gain_out, sem.at[0])]
    for piece in range(PIECES):
        for which, (source, target) in enumerate(((up_grad, up_out), (down_grad, down_out))):
            size = source.shape[0] // PIECES
            at = pl.ds(piece * size, size)
            copies.append(pltpu.make_async_copy(source.at[at, :], target.at[at, :], sem.at[2 + 2 * piece + which]))
    for copy in copies:
        copy.start()

    scaled = total[...] * f32(gain[...])
    units = unit[...]
    inner_mean = jnp.mean(scaled, axis=-1, keepdims=True)
    proj_mean = jnp.mean(scaled * units, axis=-1, keepdims=True)
    change = inverse[:, 0:1] * (scaled - inner_mean - units * proj_mean)
    input_rows[...] = (own[...] + change).astype(jnp.bfloat16)
    copies.append(pltpu.make_async_copy(input_rows, input_out, sem.at[1]))
    copies[-1].start()
    for copy in copies:
        copy.wait()


def on_device(upstream, saved_input, norm_gain, up_weight, down_weight):
    bf16, f4 = jnp.bfloat16, jnp.float32
    vmem, hbm = pl.BlockSpec(memory_space=pltpu.VMEM), pl.BlockSpec(memory_space=pl.ANY)
    dma = pltpu.SemaphoreType.DMA
    held = pl.pallas_call(
        kernel,
        out_shape=[
            pltpu.VMEM((D, HID), f4),
            pltpu.VMEM((HID, D), f4),
            pltpu.VMEM((ROWS, D), f4),
            pltpu.VMEM((ROWS, D), f4),
            pltpu.VMEM((ROWS, 128), f4),
            pltpu.VMEM((ROWS, D), f4),
            pltpu.VMEM((1, D), f4),
        ],
        in_specs=[vmem, vmem, vmem, hbm, hbm],
        out_specs=[vmem] * 7,
        scratch_shapes=[
            pltpu.VMEM((4, 4, 4, 16, D), bf16),
            pltpu.VMEM((2, 4, 4, 2, 16, HID), bf16),
            pltpu.VMEM((D, HID), bf16),
            pltpu.VMEM((4, 4, 4, 16, HALF), bf16),
            pltpu.VMEM((3, 4, 4, 16, HALF), bf16),
            pltpu.VMEM((3, 4, 16, HALF), bf16),
            pltpu.VMEM((3, 16, HALF), bf16),
            pltpu.VMEM((4, 4, 4, 16, 2 * HID), f4),
            pltpu.VMEM((16, HALF), bf16),
            pltpu.VMEM((ROWS, D), f4),
            pltpu.VMEM((3, 4, 1, D), f4),
            dma((3,)), dma((2,)),
            dma((6, 9, 3)), dma((6, 9, 3)), dma((6, 9, 3)), dma((6, 9, 3)),
            dma((3, 3)), dma((3, 3)),
        ],
        compiler_params=pltpu.CompilerParams(
            collective_id=0, has_side_effects=True, vmem_limit_bytes=42 * 2**20
        ),
        name="section_backward",
    )(upstream[0], saved_input[0], norm_gain, up_weight[0], down_weight[0].reshape(4, 4, 16, D))
    held = [pltpu.with_memory_space_constraint(array, pltpu.VMEM) for array in held]
    input_grad, gain_grad, up_grad, down_grad = pl.pallas_call(
        finish,
        out_shape=[
            jax.ShapeDtypeStruct((ROWS, D), bf16),
            jax.ShapeDtypeStruct((1, D), f4),
            jax.ShapeDtypeStruct((D, HID), f4),
            jax.ShapeDtypeStruct((HID, D), f4),
        ],
        in_specs=[vmem] * 8,
        out_specs=[hbm] * 4,
        scratch_shapes=[
            pltpu.VMEM((ROWS, D), bf16),
            dma((10,)),
        ],
        compiler_params=pltpu.CompilerParams(vmem_limit_bytes=4 * 2**20),
        name="finish",
    )(*held, norm_gain)
    return (input_grad[None], up_grad[None], down_grad[None], gain_grad)


def solution(mesh):
    in_specs = (
        P("section", ("dp", "tensor"), None),
        P("section", ("dp", "tensor"), None),
        P("section", None),
        P("section", None, ("dp", "tensor")),
        P("section", ("dp", "tensor"), None),
    )
    out_specs = (
        P("section", ("dp", "tensor"), None),
        P("section", None, ("dp", "tensor")),
        P("section", ("dp", "tensor"), None),
        P("section", None),
    )
    return jax.shard_map(
        on_device, mesh=mesh, in_specs=in_specs, out_specs=out_specs, check_vma=False
    )
```

```python
import jax
import jax.numpy as jnp
from jax import lax
from jax.experimental import pallas as pl
from jax.experimental.pallas import tpu as pltpu
from jax.sharding import PartitionSpec as P

gelu_scale = 0.7978845608028654
cubic_coef = 0.044715

D = 8192
HALF = D // 2
HID = 256
ROWS = 8
MESH = pl.DeviceIdType.MESH

ORDERS = ((2, 1, 0), (0, 2, 1), (1, 0, 2))


def cut(pieces):
    return tuple(
        (ORDERS[number // 2], 1 if number % 2 == 0 else -1, at * 128, count * 128)
        for number, (at, count) in enumerate(pieces)
    )


GATHER = cut(((0, 11), (32, 11), (11, 11), (43, 10), (22, 10), (53, 11)))
SCATTER = cut(((0, 6), (6, 5), (11, 6), (17, 5), (22, 5), (27, 5)))
SUBS = range(6)
TURNS = (0, 2, 4, 1, 3, 5)


def gelu_pair(hidden):
    tanh_part = jnp.tanh(gelu_scale * (hidden + cubic_coef * hidden * hidden * hidden))
    gelu_out = 0.5 * hidden * (1.0 + tanh_part)
    derivative = 0.5 * (1.0 + tanh_part) + 0.5 * hidden * (
        1.0 - tanh_part * tanh_part
    ) * gelu_scale * (1.0 + 3.0 * cubic_coef * hidden * hidden)
    return (gelu_out, derivative)


def f32(value):
    return value.astype(jnp.float32)


def folded(rows):
    return jnp.concatenate([rows[:, :HALF], rows[:, HALF:]], axis=0)


def apart(blocks, size):
    wide = f32(blocks).reshape(-1, 16, size)
    return tuple(half.reshape(-1, size).astype(jnp.bfloat16) for half in (wide[:, :8], wide[:, 8:]))


def kernel(
    upstream, saved, gain, up_hbm, down_hbm,
    up_grad, down_grad, total, unit, inverse, own, gain_grad,
    tokens, weights, up, part, got0, got1, got2, hid, sent_rows, gain_acc, gain_slots,
    load_sem, swap_sem, ag_send, ag_recv, rs_send, rs_recv, gain_send, gain_recv,
):
    section = lax.axis_index("section")
    dp = lax.axis_index("dp")
    tensor = lax.axis_index("tensor")
    place = (dp // 2, tensor // 2, (tensor % 2) * 2 + dp % 2)
    started = []

    def go(copy):
        copy.start()
        started.append(copy)

    def settle(count):
        for copy in started[:count]:
            copy.wait_send()
        del started[:count]

    def device_at(z, y, x):
        return (section, z * 2 + x % 2, y * 2 + x // 2)

    def moved(axis, by):
        return lax.rem(place[axis] + (by + 4), 4)

    def neighbour(axis, by):
        there = list(place)
        there[axis] = moved(axis, by)
        return device_at(*there)

    partner = (1 - section, dp, tensor)

    barrier = pltpu.get_barrier_semaphore()
    others = [neighbour(axis, by) for axis in range(3) for by in (1, 2, 3)] + [partner]
    for other in others:
        pl.semaphore_signal(barrier, inc=1, device_id=other, device_id_type=MESH)
    sent_rows[...] = folded(f32(upstream[...])).astype(jnp.bfloat16)
    rows = f32(saved[...])
    centered = rows - jnp.mean(rows, axis=-1, keepdims=True)
    spread = lax.rsqrt(jnp.mean(centered * centered, axis=-1, keepdims=True) + 1e-05)
    inverse[...] = jnp.broadcast_to(spread, inverse.shape)
    unit[...] = centered * spread
    tokens[place[0], place[1], place[2], :, 0:HALF] = folded(unit[...] * f32(gain[...])).astype(jnp.bfloat16)
    pl.semaphore_wait(barrier, len(others))

    swap = pltpu.make_async_remote_copy(
        src_ref=sent_rows, dst_ref=tokens.at[place[0], place[1], place[2], :, pl.ds(HALF, HALF)],
        send_sem=swap_sem.at[0], recv_sem=swap_sem.at[1], device_id=partner, device_id_type=MESH,
    )
    go(swap)

    def gathered(phase, sub, unit_by, where):
        order, _, lo, size = GATHER[sub]
        index = [slice(None)] * 3
        for later in range(phase, 3):
            index[order[later]] = place[order[later]]
        if phase:
            index[order[phase - 1]] = moved(order[phase - 1], unit_by)
        index[order[phase]] = where
        return tokens.at[(*index, slice(None), pl.ds(lo, size))]

    def slot(phase, unit_by):
        return 0 if phase == 0 else 4 * phase - 3 + unit_by % 4

    def ag_copy(phase, sub, unit_by, message, where, by):
        block = gathered(phase, sub, unit_by, where)
        return pltpu.make_async_remote_copy(
            src_ref=block, dst_ref=block,
            send_sem=ag_send.at[sub, slot(phase, unit_by), message],
            recv_sem=ag_recv.at[sub, slot(phase, unit_by), message],
            device_id=neighbour(GATHER[sub][0][phase], by), device_id_type=MESH,
        )

    def ag_start(phase, sub, unit_by=0):
        axis, way = GATHER[sub][0][phase], GATHER[sub][1]
        go(ag_copy(phase, sub, unit_by, 0, place[axis], way))
        go(ag_copy(phase, sub, unit_by, 1, place[axis], -way))

    def ag_forward(phase, sub, unit_by=0):
        axis, way = GATHER[sub][0][phase], GATHER[sub][1]
        ag_copy(phase, sub, unit_by, 0, moved(axis, -way), way).wait_recv()
        go(ag_copy(phase, sub, unit_by, 2, moved(axis, -way), way))

    def ag_wait(phase, sub, message, unit_by=0):
        axis, way = GATHER[sub][0][phase], GATHER[sub][1]
        ag_copy(phase, sub, unit_by, message, moved(axis, way if message == 1 else 2), way).wait_recv()

    def plane(order, where):
        index = [slice(None)] * 3
        index[order[2]] = where
        return tuple(index)

    def first_products(sub, by, lines=None):
        order, _, lo, size = GATHER[sub]
        places = []
        for line in (None,) if lines is None else lines:
            at = list(plane(order, moved(order[2], by)))
            if line is not None:
                at[order[1]] = moved(order[1], line)
            places.append(tuple(at))
        blocks = [tokens[(*at, slice(None), pl.ds(lo, size))].reshape(-1, 16, size) for at in places]
        halves = apart(blocks[0] if len(blocks) == 1 else jnp.concatenate(blocks, axis=0), size)
        products = []
        for half, rows in enumerate(halves):
            if sub % 2 == 0:
                matrix, dims = up[pl.ds(half * HALF + lo, size), :], (((1,), (0,)), ((), ()))
            else:
                matrix = part[half, :, :, :, pl.ds(lo - HALF, size)].reshape(HID, size)
                dims = (((1,), (1,)), ((), ()))
            products.append(lax.dot_general(rows, matrix, dims, preferred_element_type=jnp.float32))
        summed = products[0] + products[1]
        count = summed.shape[0] // len(places)
        shape = ((4, 4) if lines is None else (4,)) + (8, HID)
        corner = (pl.ds(0, 8), pl.ds(0, HID)) if sub % 2 == 0 else (pl.ds(8, 8), pl.ds(HID, HID))
        for turn, at in enumerate(places):
            hid[(*at, *corner)] += summed[turn * count : (turn + 1) * count].reshape(shape)

    def way_of(sub):
        return GATHER[sub][1]

    for half in range(2):
        if half:
            swap.wait_recv()
        for sub in SUBS[half::2]:
            ag_start(0, sub)
        for sub in SUBS[half::2]:
            ag_start(1, sub, 0)
    load_up = pltpu.make_async_copy(up_hbm, up, load_sem.at[0])
    load_down = [
        pltpu.make_async_copy(down_hbm.at[:, :, :, pl.ds(half * HALF, HALF)], part.at[half], load_sem.at[1 + half])
        for half in range(2)
    ]
    load_up.start()
    for load in load_down:
        load.start()
    hid[...] = jnp.zeros_like(hid)
    for sub in TURNS:
        ag_forward(0, sub)
        ag_start(1, sub, -way_of(sub))
    for sub in TURNS:
        ag_wait(0, sub, 1)
        ag_start(1, sub, way_of(sub))
    for sub in TURNS:
        ag_forward(1, sub, 0)
    for sub in TURNS:
        ag_wait(0, sub, 2)
        ag_start(1, sub, 2)
        ag_start(2, sub, 0)
    for sub in TURNS:
        ag_forward(1, sub, -way_of(sub))
    for sub in TURNS:
        ag_forward(1, sub, way_of(sub))
    for sub in TURNS:
        ag_forward(1, sub, 2)
        ag_start(2, sub, -way_of(sub))
    for sub in TURNS:
        for unit_by in range(4):
            ag_wait(1, sub, 1, unit_by)
        ag_start(2, sub, way_of(sub))
    for sub in TURNS:
        for unit_by in range(4):
            ag_wait(1, sub, 2, unit_by)
        ag_start(2, sub, 2)
    load_up.wait()
    for load in load_down:
        load.wait()
    for sub in TURNS:
        ag_forward(2, sub, 0)
    for sub in TURNS:
        first_products(sub, 0)
    for sub in TURNS:
        ag_forward(2, sub, -way_of(sub))
    for sub in TURNS:
        ag_forward(2, sub, way_of(sub))
    for sub in TURNS:
        ag_forward(2, sub, 2)
    for sub in TURNS:
        first_products(sub, -way_of(sub))
    for sub in TURNS:
        for unit_by in range(4):
            ag_wait(2, sub, 1, unit_by)
        first_products(sub, way_of(sub))
    for unit_by in (0, 1, 3):
        for sub in TURNS:
            ag_wait(2, sub, 2, unit_by)
    for sub in TURNS:
        first_products(sub, 2, (0, 1, -1))
    for sub in TURNS:
        ag_wait(2, sub, 2, 2)
        first_products(sub, 2, (2,))

    SWAPPED = (0, 2, 1, 3)

    def activate(z, carry):
        for y in range(4):
            act, derivative = gelu_pair(hid[z, y, :, 0:8, 0:HID])
            for x in range(4):
                hid[z, y, x, 0:8, HID:] = hid[y, z, SWAPPED[x], 8:16, HID:] * derivative[x]
                hid[z, y, x, 0:8, 0:HID] = act[x]
        return carry

    lax.fori_loop(0, 4, activate, 0)
    gathers = len(started)

    def lay_out(step, carry):
        z, y = step // 4, step % 4
        for pair in range(2):
            first, second = 2 * pair, 2 * pair + 1
            weights[0, z, y, pair] = jnp.concatenate(
                [hid[z, y, x, 0:8, HID:] for x in (first, second)], axis=0
            ).astype(jnp.bfloat16)
            weights[1, z, y, pair] = jnp.concatenate(
                [hid[y, z, SWAPPED[x], 0:8, 0:HID] for x in (first, second)], axis=0
            ).astype(jnp.bfloat16)
        return carry

    def second_products(sub, by):
        order, _, lo, size = SCATTER[sub]
        at = plane(order, moved(order[2], by))
        left = hid[(*at, pl.ds(0, 8), pl.ds(HID, HID))].reshape(128, HID).astype(jnp.bfloat16)
        halves = []
        for start in (lo, HALF + lo):
            halves.append(
                lax.dot_general(
                    left, up[pl.ds(start, size), :], (((1,), (1,)), ((), ())), preferred_element_type=jnp.float32
                ).reshape(4, 4, 8, size)
            )
        part[(*at, slice(None), pl.ds(lo, size))] = jnp.concatenate(halves, axis=2).astype(jnp.bfloat16)

    def two_axes(order, b_index, a_index=slice(None)):
        return tuple(b_index if axis == order[1] else a_index for axis in range(3) if axis != order[2])

    def landing(phase, sub, unit_by, message):
        order, _, lo, size = SCATTER[sub]
        columns = (slice(None), pl.ds(lo, size))
        if phase == 0:
            return got0.at[(message, *two_axes(order, moved(order[1], unit_by)), *columns)]
        return got1.at[(message, moved(order[0], unit_by), *columns)]

    def share(phase, sub, unit_by, by):
        order, _, lo, size = SCATTER[sub]
        columns = (slice(None), pl.ds(lo, size))
        where = moved(order[2 - phase], by)
        if phase == 0:
            index = list(plane(order, where))
            index[order[1]] = moved(order[1], unit_by)
            return part.at[(*index, *columns)]
        return got0.at[(2, *two_axes(order, where, moved(order[0], unit_by)), *columns)]

    def rs_copy(phase, sub, unit_by, message):
        order, way = SCATTER[sub][0], SCATTER[sub][1]
        if message == 0:
            source, by = share(phase, sub, unit_by, 2), -way
        elif message == 1:
            source, by = share(phase, sub, unit_by, way), way
        else:
            source, by = landing(phase, sub, unit_by, 0), -way
        at = slot(2 - phase, unit_by)
        return pltpu.make_async_remote_copy(
            src_ref=source, dst_ref=landing(phase, sub, unit_by, message),
            send_sem=rs_send.at[sub, at, message], recv_sem=rs_recv.at[sub, at, message],
            device_id=neighbour(order[2 - phase], by), device_id_type=MESH,
        )

    def rs_start(phase, sub, unit_by, message):
        go(rs_copy(phase, sub, unit_by, message))

    def rs_forward(phase, sub, unit_by=0):
        rs_copy(phase, sub, unit_by, 0).wait_recv()
        ref = landing(phase, sub, unit_by, 0)
        mine = share(phase, sub, unit_by, -way_of(sub))
        ref[...] = (f32(ref[...]) + f32(mine[...])).astype(jnp.bfloat16)
        rs_start(phase, sub, unit_by, 2)

    def rs_sum(phase, sub, unit_by=0):
        rs_copy(phase, sub, unit_by, 1).wait_recv()
        rs_copy(phase, sub, unit_by, 2).wait_recv()
        mine = share(phase, sub, unit_by, 0)
        ref = landing(phase, sub, unit_by, 2)
        summed = f32(mine[...]) + f32(landing(phase, sub, unit_by, 1)[...]) + f32(ref[...])
        ref[...] = summed.astype(jnp.bfloat16)

    def last_copy(sub, by):
        order, _, lo, size = SCATTER[sub]
        columns = (slice(None), pl.ds(lo, size))
        return pltpu.make_async_remote_copy(
            src_ref=got1.at[(2, moved(order[0], by), *columns)], dst_ref=got2.at[(by - 1, *columns)],
            send_sem=rs_send.at[sub, 0, by - 1], recv_sem=rs_recv.at[sub, 0, by - 1],
            device_id=neighbour(order[0], by), device_id_type=MESH,
        )

    def far_first(sub):
        return (2, way_of(sub), -way_of(sub), 0)

    for sub in SUBS:
        second_products(sub, 2)
        for turn in (0, 1):
            rs_start(0, sub, far_first(sub)[turn], 0)
    for sub in SUBS:
        second_products(sub, way_of(sub))
        for turn in (0, 1):
            rs_start(0, sub, far_first(sub)[turn], 1)
    for sub in SUBS:
        second_products(sub, -way_of(sub))

    def line_step(turn):
        for sub in SUBS:
            rs_forward(0, sub, far_first(sub)[turn])
            if turn < 2:
                rs_start(0, sub, far_first(sub)[turn + 2], 0)
            if 0 < turn < 3:
                rs_start(0, sub, far_first(sub)[turn + 1], 1)

    def line_sum(turn):
        for sub in SUBS:
            rs_sum(0, sub, far_first(sub)[turn])
            if turn < 2:
                for unit_by in far_first(sub):
                    rs_start(1, sub, unit_by, turn)

    TILE = 256

    def weight_tile(step, carry):
        normed_at = pl.ds(pl.multiple_of(step * TILE, TILE), TILE)
        grad_at = pl.ds(pl.multiple_of(HALF + step * TILE, TILE), TILE)
        for half, rows in enumerate(apart(tokens[:, :, :, :, normed_at], TILE)):
            up_grad[pl.ds(pl.multiple_of(half * HALF + step * TILE, TILE), TILE), :] = lax.dot_general(
                rows, weights[0].reshape(512, HID), (((0,), (0,)), ((), ())), preferred_element_type=jnp.float32
            )
        for half, rows in enumerate(apart(tokens[:, :, :, :, grad_at], TILE)):
            down_grad[:, pl.ds(pl.multiple_of(half * HALF + step * TILE, TILE), TILE)] = lax.dot_general(
                weights[1].reshape(512, HID), rows, (((0,), (0,)), ((), ())), preferred_element_type=jnp.float32
            )
        return carry

    lax.fori_loop(0, 16, lay_out, 0)
    lax.fori_loop(0, 4, weight_tile, 0)
    line_step(0)
    settle(gathers)
    line_step(1)
    early = len(started)
    for sub in SUBS:
        second_products(sub, 0)
    line_sum(0)
    line_step(2)

    def gain_tile(step, carry):
        at = pl.ds(pl.multiple_of(step * 256, 256), 256)
        also = pl.ds(pl.multiple_of(HALF + step * 256, 256), 256)
        sums = jnp.zeros((16, 256), jnp.float32)
        for z in range(4):
            sums = sums + jnp.sum((f32(part[z, :, :, :, at]) * f32(tokens[z, :, :, :, at])).reshape(16, 16, 256), axis=0)
        gain_acc[:, at] = sums[:8]
        gain_acc[:, also] = sums[8:]
        return carry

    lax.fori_loop(0, HALF // 256, gain_tile, 0)
    gain_slots[0, place[2]] = jnp.sum(gain_acc[...], axis=0, keepdims=True) / f32(gain[...])

    def gain_copy(phase, by, owner):
        axis = 2 - phase
        return pltpu.make_async_remote_copy(
            src_ref=gain_slots.at[phase, owner], dst_ref=gain_slots.at[phase, owner],
            send_sem=gain_send.at[phase, by - 1], recv_sem=gain_recv.at[phase, by - 1],
            device_id=neighbour(axis, by), device_id_type=MESH,
        )

    def gain_start(phase):
        for by in (1, 2, 3):
            go(gain_copy(phase, by, place[2 - phase]))

    def gain_sum(phase):
        for by in (1, 2, 3):
            gain_copy(phase, by, moved(2 - phase, -by)).wait_recv()
        return (gain_slots[phase, 0] + gain_slots[phase, 1]) + (gain_slots[phase, 2] + gain_slots[phase, 3])

    gain_start(0)
    line_sum(1)
    line_step(3)
    lax.fori_loop(4, 10, weight_tile, 0)
    settle(early)
    gain_slots[1, place[1]] = gain_sum(0)
    gain_start(1)
    line_sum(2)
    for turn in range(4):
        for sub in SUBS:
            rs_forward(1, sub, far_first(sub)[turn])
    sent = len(started)
    lax.fori_loop(10, 14, weight_tile, 0)
    gain_slots[2, place[0]] = gain_sum(1)
    gain_start(2)
    line_sum(3)
    for turn in range(3):
        for sub in SUBS:
            unit_by = far_first(sub)[turn]
            rs_sum(1, sub, unit_by)
            go(last_copy(sub, unit_by % 4))
    for sub in SUBS:
        rs_sum(1, sub, 0)
    lax.fori_loop(14, 16, weight_tile, 0)
    settle(sent)
    gain_grad[...] = gain_sum(2)
    kept = f32(tokens[place[1], place[0], (place[2] % 2) * 2 + place[2] // 2, :, HALF:])
    own[:, :HALF] = kept[:8]
    own[:, HALF:] = kept[8:]
    for sub in SUBS:
        _, _, lo, size = SCATTER[sub]
        for by in (1, 2, 3):
            last_copy(sub, by).wait_recv()
        columns = (slice(None), pl.ds(lo, size))
        summed = f32(got1[(2, place[SCATTER[sub][0][0]], *columns)])
        for by in (1, 2, 3):
            summed = summed + f32(got2[(by - 1, *columns)])
        total[:, pl.ds(lo, size)] = summed[:8]
        total[:, pl.ds(HALF + lo, size)] = summed[8:]
    settle(len(started))


def finish(
    up_grad, down_grad, total, unit, inverse, own, gain_grad, gain,
    input_out, gain_out, up_out, down_out,
    input_rows, sem,
):
    PIECES = 4
    copies = [pltpu.make_async_copy(gain_grad, gain_out, sem.at[0])]
    for piece in range(PIECES):
        for which, (source, target) in enumerate(((up_grad, up_out), (down_grad, down_out))):
            size = source.shape[0] // PIECES
            at = pl.ds(piece * size, size)
            copies.append(pltpu.make_async_copy(source.at[at, :], target.at[at, :], sem.at[2 + 2 * piece + which]))
    for copy in copies:
        copy.start()

    scaled = total[...] * f32(gain[...])
    units = unit[...]
    inner_mean = jnp.mean(scaled, axis=-1, keepdims=True)
    proj_mean = jnp.mean(scaled * units, axis=-1, keepdims=True)
    change = inverse[:, 0:1] * (scaled - inner_mean - units * proj_mean)
    input_rows[...] = (own[...] + change).astype(jnp.bfloat16)
    copies.append(pltpu.make_async_copy(input_rows, input_out, sem.at[1]))
    copies[-1].start()
    for copy in copies:
        copy.wait()


def on_device(upstream, saved_input, norm_gain, up_weight, down_weight):
    bf16, f4 = jnp.bfloat16, jnp.float32
    vmem, hbm = pl.BlockSpec(memory_space=pltpu.VMEM), pl.BlockSpec(memory_space=pl.ANY)
    dma = pltpu.SemaphoreType.DMA
    held = pl.pallas_call(
        kernel,
        out_shape=[
            pltpu.VMEM((D, HID), f4),
            pltpu.VMEM((HID, D), f4),
            pltpu.VMEM((ROWS, D), f4),
            pltpu.VMEM((ROWS, D), f4),
            pltpu.VMEM((ROWS, 128), f4),
            pltpu.VMEM((ROWS, D), f4),
            pltpu.VMEM((1, D), f4),
        ],
        in_specs=[vmem, vmem, vmem, hbm, hbm],
        out_specs=[vmem] * 7,
        scratch_shapes=[
            pltpu.VMEM((4, 4, 4, 16, D), bf16),
            pltpu.VMEM((2, 4, 4, 2, 16, HID), bf16),
            pltpu.VMEM((D, HID), bf16),
            pltpu.VMEM((4, 4, 4, 16, HALF), bf16),
            pltpu.VMEM((3, 4, 4, 16, HALF), bf16),
            pltpu.VMEM((3, 4, 16, HALF), bf16),
            pltpu.VMEM((3, 16, HALF), bf16),
            pltpu.VMEM((4, 4, 4, 16, 2 * HID), f4),
            pltpu.VMEM((16, HALF), bf16),
            pltpu.VMEM((ROWS, D), f4),
            pltpu.VMEM((3, 4, 1, D), f4),
            dma((3,)), dma((2,)),
            dma((6, 9, 3)), dma((6, 9, 3)), dma((6, 9, 3)), dma((6, 9, 3)),
            dma((3, 3)), dma((3, 3)),
        ],
        compiler_params=pltpu.CompilerParams(
            collective_id=0, has_side_effects=True, vmem_limit_bytes=42 * 2**20
        ),
        name="section_backward",
    )(upstream[0], saved_input[0], norm_gain, up_weight[0], down_weight[0].reshape(4, 4, 16, D))
    held = [pltpu.with_memory_space_constraint(array, pltpu.VMEM) for array in held]
    input_grad, gain_grad, up_grad, down_grad = pl.pallas_call(
        finish,
        out_shape=[
            jax.ShapeDtypeStruct((ROWS, D), bf16),
            jax.ShapeDtypeStruct((1, D), f4),
            jax.ShapeDtypeStruct((D, HID), f4),
            jax.ShapeDtypeStruct((HID, D), f4),
        ],
        in_specs=[vmem] * 8,
        out_specs=[hbm] * 4,
        scratch_shapes=[
            pltpu.VMEM((ROWS, D), bf16),
            dma((10,)),
        ],
        compiler_params=pltpu.CompilerParams(vmem_limit_bytes=4 * 2**20),
        name="finish",
    )(*held, norm_gain)
    return (input_grad[None], up_grad[None], down_grad[None], gain_grad)


def solution(mesh):
    in_specs = (
        P("section", ("dp", "tensor"), None),
        P("section", ("dp", "tensor"), None),
        P("section", None),
        P("section", None, ("dp", "tensor")),
        P("section", ("dp", "tensor"), None),
    )
    out_specs = (
        P("section", ("dp", "tensor"), None),
        P("section", None, ("dp", "tensor")),
        P("section", ("dp", "tensor"), None),
        P("section", None),
    )
    return jax.shard_map(
        on_device, mesh=mesh, in_specs=in_specs, out_specs=out_specs, check_vma=False
    )
```

```python
import jax
import jax.numpy as jnp
from jax import lax
from jax.experimental import pallas as pl
from jax.experimental.pallas import tpu as pltpu
from jax.sharding import PartitionSpec as P

gelu_scale = 0.7978845608028654
cubic_coef = 0.044715

D = 8192
HALF = D // 2
HID = 256
ROWS = 8
MESH = pl.DeviceIdType.MESH

ORDERS = ((2, 1, 0), (0, 2, 1), (1, 0, 2))


def cut(pieces):
    return tuple(
        (ORDERS[number // 2], 1 if number % 2 == 0 else -1, at * 128, count * 128)
        for number, (at, count) in enumerate(pieces)
    )


GATHER = cut(((0, 11), (32, 11), (11, 11), (43, 10), (22, 10), (53, 11)))
SCATTER = cut(((0, 6), (6, 5), (11, 6), (17, 5), (22, 5), (27, 5)))
SUBS = range(6)
TURNS = (0, 2, 4, 1, 3, 5)


def gelu_pair(hidden):
    tanh_part = jnp.tanh(gelu_scale * (hidden + cubic_coef * hidden * hidden * hidden))
    gelu_out = 0.5 * hidden * (1.0 + tanh_part)
    derivative = 0.5 * (1.0 + tanh_part) + 0.5 * hidden * (
        1.0 - tanh_part * tanh_part
    ) * gelu_scale * (1.0 + 3.0 * cubic_coef * hidden * hidden)
    return (gelu_out, derivative)


def f32(value):
    return value.astype(jnp.float32)


def folded(rows):
    return jnp.concatenate([rows[:, :HALF], rows[:, HALF:]], axis=0)


def apart(blocks, size):
    wide = f32(blocks).reshape(-1, 16, size)
    return tuple(half.reshape(-1, size).astype(jnp.bfloat16) for half in (wide[:, :8], wide[:, 8:]))


def kernel(
    upstream, saved, gain, up_hbm, down_hbm,
    up_grad, down_grad, total, unit, inverse, own, gain_grad,
    tokens, weights, up, part, got0, got1, got2, hid, sent_rows, gain_acc, gain_slots,
    load_sem, swap_sem, ag_send, ag_recv, rs_send, rs_recv, gain_send, gain_recv,
):
    section = lax.axis_index("section")
    dp = lax.axis_index("dp")
    tensor = lax.axis_index("tensor")
    place = (dp // 2, tensor // 2, (tensor % 2) * 2 + dp % 2)
    started = []

    def go(copy):
        copy.start()
        started.append(copy)

    def settle(count):
        for copy in started[:count]:
            copy.wait_send()
        del started[:count]

    def device_at(z, y, x):
        return (section, z * 2 + x % 2, y * 2 + x // 2)

    def moved(axis, by):
        return lax.rem(place[axis] + (by + 4), 4)

    def neighbour(axis, by):
        there = list(place)
        there[axis] = moved(axis, by)
        return device_at(*there)

    partner = (1 - section, dp, tensor)

    barrier = pltpu.get_barrier_semaphore()
    others = [neighbour(axis, by) for axis in range(3) for by in (1, 2, 3)] + [partner]
    for other in others:
        pl.semaphore_signal(barrier, inc=1, device_id=other, device_id_type=MESH)
    sent_rows[...] = folded(f32(upstream[...])).astype(jnp.bfloat16)
    rows = f32(saved[...])
    centered = rows - jnp.mean(rows, axis=-1, keepdims=True)
    spread = lax.rsqrt(jnp.mean(centered * centered, axis=-1, keepdims=True) + 1e-05)
    inverse[...] = jnp.broadcast_to(spread, inverse.shape)
    unit[...] = centered * spread
    tokens[place[0], place[1], place[2], :, 0:HALF] = folded(unit[...] * f32(gain[...])).astype(jnp.bfloat16)
    pl.semaphore_wait(barrier, len(others))

    swap = pltpu.make_async_remote_copy(
        src_ref=sent_rows, dst_ref=tokens.at[place[0], place[1], place[2], :, pl.ds(HALF, HALF)],
        send_sem=swap_sem.at[0], recv_sem=swap_sem.at[1], device_id=partner, device_id_type=MESH,
    )
    go(swap)

    def gathered(phase, sub, unit_by, where):
        order, _, lo, size = GATHER[sub]
        index = [slice(None)] * 3
        for later in range(phase, 3):
            index[order[later]] = place[order[later]]
        if phase:
            index[order[phase - 1]] = moved(order[phase - 1], unit_by)
        index[order[phase]] = where
        return tokens.at[(*index, slice(None), pl.ds(lo, size))]

    def slot(phase, unit_by):
        return 0 if phase == 0 else 4 * phase - 3 + unit_by % 4

    def ag_copy(phase, sub, unit_by, message, where, by):
        block = gathered(phase, sub, unit_by, where)
        return pltpu.make_async_remote_copy(
            src_ref=block, dst_ref=block,
            send_sem=ag_send.at[sub, slot(phase, unit_by), message],
            recv_sem=ag_recv.at[sub, slot(phase, unit_by), message],
            device_id=neighbour(GATHER[sub][0][phase], by), device_id_type=MESH,
        )

    def ag_start(phase, sub, unit_by=0):
        axis, way = GATHER[sub][0][phase], GATHER[sub][1]
        go(ag_copy(phase, sub, unit_by, 0, place[axis], way))
        go(ag_copy(phase, sub, unit_by, 1, place[axis], -way))

    def ag_forward(phase, sub, unit_by=0):
        axis, way = GATHER[sub][0][phase], GATHER[sub][1]
        ag_copy(phase, sub, unit_by, 0, moved(axis, -way), way).wait_recv()
        go(ag_copy(phase, sub, unit_by, 2, moved(axis, -way), way))

    def ag_wait(phase, sub, message, unit_by=0):
        axis, way = GATHER[sub][0][phase], GATHER[sub][1]
        ag_copy(phase, sub, unit_by, message, moved(axis, way if message == 1 else 2), way).wait_recv()

    def plane(order, where):
        index = [slice(None)] * 3
        index[order[2]] = where
        return tuple(index)

    def first_products(sub, by, lines=None):
        order, _, lo, size = GATHER[sub]
        places = []
        for line in (None,) if lines is None else lines:
            at = list(plane(order, moved(order[2], by)))
            if line is not None:
                at[order[1]] = moved(order[1], line)
            places.append(tuple(at))
        blocks = [tokens[(*at, slice(None), pl.ds(lo, size))].reshape(-1, 16, size) for at in places]
        halves = apart(blocks[0] if len(blocks) == 1 else jnp.concatenate(blocks, axis=0), size)
        products = []
        for half, rows in enumerate(halves):
            if sub % 2 == 0:
                matrix, dims = up[pl.ds(half * HALF + lo, size), :], (((1,), (0,)), ((), ()))
            else:
                matrix = part[half, :, :, :, pl.ds(lo - HALF, size)].reshape(HID, size)
                dims = (((1,), (1,)), ((), ()))
            products.append(lax.dot_general(rows, matrix, dims, preferred_element_type=jnp.float32))
        summed = products[0] + products[1]
        count = summed.shape[0] // len(places)
        shape = ((4, 4) if lines is None else (4,)) + (8, HID)
        corner = (pl.ds(0, 8), pl.ds(0, HID)) if sub % 2 == 0 else (pl.ds(8, 8), pl.ds(HID, HID))
        for turn, at in enumerate(places):
            hid[(*at, *corner)] += summed[turn * count : (turn + 1) * count].reshape(shape)

    def way_of(sub):
        return GATHER[sub][1]

    for half in range(2):
        if half:
            swap.wait_recv()
        for sub in SUBS[half::2]:
            ag_start(0, sub)
        for sub in SUBS[half::2]:
            ag_start(1, sub, 0)
    load_up = pltpu.make_async_copy(up_hbm, up, load_sem.at[0])
    load_down = [
        pltpu.make_async_copy(down_hbm.at[:, :, :, pl.ds(half * HALF, HALF)], part.at[half], load_sem.at[1 + half])
        for half in range(2)
    ]
    load_up.start()
    for load in load_down:
        load.start()
    hid[...] = jnp.zeros_like(hid)
    for sub in TURNS:
        ag_forward(0, sub)
        ag_start(1, sub, -way_of(sub))
    for sub in TURNS:
        ag_wait(0, sub, 1)
        ag_start(1, sub, way_of(sub))
    for sub in TURNS:
        ag_forward(1, sub, 0)
    for sub in TURNS:
        ag_wait(0, sub, 2)
        ag_start(1, sub, 2)
        ag_start(2, sub, 0)
    for sub in TURNS:
        ag_forward(1, sub, -way_of(sub))
    for sub in TURNS:
        ag_forward(1, sub, way_of(sub))
    for sub in TURNS:
        ag_forward(1, sub, 2)
        ag_start(2, sub, -way_of(sub))
    for sub in TURNS:
        for unit_by in range(4):
            ag_wait(1, sub, 1, unit_by)
        ag_start(2, sub, way_of(sub))
    for sub in TURNS:
        for unit_by in range(4):
            ag_wait(1, sub, 2, unit_by)
        ag_start(2, sub, 2)
    load_up.wait()
    for load in load_down:
        load.wait()
    for sub in TURNS:
        ag_forward(2, sub, 0)
    for sub in TURNS:
        first_products(sub, 0)
    for sub in TURNS:
        ag_forward(2, sub, -way_of(sub))
    for sub in TURNS:
        ag_forward(2, sub, way_of(sub))
    for sub in TURNS:
        ag_forward(2, sub, 2)
    for sub in TURNS:
        first_products(sub, -way_of(sub))
    for sub in TURNS:
        for unit_by in range(4):
            ag_wait(2, sub, 1, unit_by)
        first_products(sub, way_of(sub))
    for unit_by in (0, 1, 3):
        for sub in TURNS:
            ag_wait(2, sub, 2, unit_by)
    for sub in TURNS:
        first_products(sub, 2, (0, 1, -1))
    for sub in TURNS:
        ag_wait(2, sub, 2, 2)
        first_products(sub, 2, (2,))

    SWAPPED = (0, 2, 1, 3)

    def activate(z, carry):
        for y in range(4):
            act, derivative = gelu_pair(hid[z, y, :, 0:8, 0:HID])
            for x in range(4):
                hid[z, y, x, 0:8, HID:] = hid[y, z, SWAPPED[x], 8:16, HID:] * derivative[x]
                hid[z, y, x, 0:8, 0:HID] = act[x]
        return carry

    lax.fori_loop(0, 4, activate, 0)
    gathers = len(started)

    def lay_out(step, carry):
        z, y = step // 4, step % 4
        for pair in range(2):
            first, second = 2 * pair, 2 * pair + 1
            weights[0, z, y, pair] = jnp.concatenate(
                [hid[z, y, x, 0:8, HID:] for x in (first, second)], axis=0
            ).astype(jnp.bfloat16)
            weights[1, z, y, pair] = jnp.concatenate(
                [hid[y, z, SWAPPED[x], 0:8, 0:HID] for x in (first, second)], axis=0
            ).astype(jnp.bfloat16)
        return carry

    def second_products(sub, by):
        order, _, lo, size = SCATTER[sub]
        at = plane(order, moved(order[2], by))
        left = hid[(*at, pl.ds(0, 8), pl.ds(HID, HID))].reshape(128, HID).astype(jnp.bfloat16)
        halves = []
        for start in (lo, HALF + lo):
            halves.append(
                lax.dot_general(
                    left, up[pl.ds(start, size), :], (((1,), (1,)), ((), ())), preferred_element_type=jnp.float32
                ).reshape(4, 4, 8, size)
            )
        part[(*at, slice(None), pl.ds(lo, size))] = jnp.concatenate(halves, axis=2).astype(jnp.bfloat16)

    def two_axes(order, b_index, a_index=slice(None)):
        return tuple(b_index if axis == order[1] else a_index for axis in range(3) if axis != order[2])

    def landing(phase, sub, unit_by, message):
        order, _, lo, size = SCATTER[sub]
        columns = (slice(None), pl.ds(lo, size))
        if phase == 0:
            return got0.at[(message, *two_axes(order, moved(order[1], unit_by)), *columns)]
        return got1.at[(message, moved(order[0], unit_by), *columns)]

    def share(phase, sub, unit_by, by):
        order, _, lo, size = SCATTER[sub]
        columns = (slice(None), pl.ds(lo, size))
        where = moved(order[2 - phase], by)
        if phase == 0:
            index = list(plane(order, where))
            index[order[1]] = moved(order[1], unit_by)
            return part.at[(*index, *columns)]
        return got0.at[(2, *two_axes(order, where, moved(order[0], unit_by)), *columns)]

    def rs_copy(phase, sub, unit_by, message):
        order, way = SCATTER[sub][0], SCATTER[sub][1]
        if message == 0:
            source, by = share(phase, sub, unit_by, 2), -way
        elif message == 1:
            source, by = share(phase, sub, unit_by, way), way
        else:
            source, by = landing(phase, sub, unit_by, 0), -way
        at = slot(2 - phase, unit_by)
        return pltpu.make_async_remote_copy(
            src_ref=source, dst_ref=landing(phase, sub, unit_by, message),
            send_sem=rs_send.at[sub, at, message], recv_sem=rs_recv.at[sub, at, message],
            device_id=neighbour(order[2 - phase], by), device_id_type=MESH,
        )

    def rs_start(phase, sub, unit_by, message):
        go(rs_copy(phase, sub, unit_by, message))

    def rs_forward(phase, sub, unit_by=0):
        rs_copy(phase, sub, unit_by, 0).wait_recv()
        ref = landing(phase, sub, unit_by, 0)
        mine = share(phase, sub, unit_by, -way_of(sub))
        ref[...] = (f32(ref[...]) + f32(mine[...])).astype(jnp.bfloat16)
        rs_start(phase, sub, unit_by, 2)

    def rs_sum(phase, sub, unit_by=0):
        rs_copy(phase, sub, unit_by, 1).wait_recv()
        rs_copy(phase, sub, unit_by, 2).wait_recv()
        mine = share(phase, sub, unit_by, 0)
        ref = landing(phase, sub, unit_by, 2)
        summed = f32(mine[...]) + f32(landing(phase, sub, unit_by, 1)[...]) + f32(ref[...])
        ref[...] = summed.astype(jnp.bfloat16)

    def last_copy(sub, by):
        order, _, lo, size = SCATTER[sub]
        columns = (slice(None), pl.ds(lo, size))
        return pltpu.make_async_remote_copy(
            src_ref=got1.at[(2, moved(order[0], by), *columns)], dst_ref=got2.at[(by - 1, *columns)],
            send_sem=rs_send.at[sub, 0, by - 1], recv_sem=rs_recv.at[sub, 0, by - 1],
            device_id=neighbour(order[0], by), device_id_type=MESH,
        )

    def far_first(sub):
        return (2, way_of(sub), -way_of(sub), 0)

    for sub in SUBS:
        second_products(sub, 2)
        for turn in (0, 1):
            rs_start(0, sub, far_first(sub)[turn], 0)
    for sub in SUBS:
        second_products(sub, way_of(sub))
        for turn in (0, 1):
            rs_start(0, sub, far_first(sub)[turn], 1)
    for sub in SUBS:
        second_products(sub, -way_of(sub))

    def line_step(turn):
        for sub in SUBS:
            if turn < 2:
                rs_start(0, sub, far_first(sub)[turn + 2], 0)
            if 0 < turn < 3:
                rs_start(0, sub, far_first(sub)[turn + 1], 1)
        for sub in SUBS:
            rs_forward(0, sub, far_first(sub)[turn])

    def line_sum(turn):
        for sub in SUBS:
            rs_sum(0, sub, far_first(sub)[turn])
            if turn < 2:
                for unit_by in far_first(sub):
                    rs_start(1, sub, unit_by, turn)

    TILE = 256

    def weight_tile(step, carry):
        normed_at = pl.ds(pl.multiple_of(step * TILE, TILE), TILE)
        grad_at = pl.ds(pl.multiple_of(HALF + step * TILE, TILE), TILE)
        for half, rows in enumerate(apart(tokens[:, :, :, :, normed_at], TILE)):
            up_grad[pl.ds(pl.multiple_of(half * HALF + step * TILE, TILE), TILE), :] = lax.dot_general(
                rows, weights[0].reshape(512, HID), (((0,), (0,)), ((), ())), preferred_element_type=jnp.float32
            )
        for half, rows in enumerate(apart(tokens[:, :, :, :, grad_at], TILE)):
            down_grad[:, pl.ds(pl.multiple_of(half * HALF + step * TILE, TILE), TILE)] = lax.dot_general(
                weights[1].reshape(512, HID), rows, (((0,), (0,)), ((), ())), preferred_element_type=jnp.float32
            )
        return carry

    lax.fori_loop(0, 16, lay_out, 0)
    lax.fori_loop(0, 4, weight_tile, 0)
    line_step(0)
    settle(gathers)
    line_step(1)
    early = len(started)
    for sub in SUBS:
        second_products(sub, 0)
    line_sum(0)
    line_step(2)

    def gain_tile(step, carry):
        at = pl.ds(pl.multiple_of(step * 256, 256), 256)
        also = pl.ds(pl.multiple_of(HALF + step * 256, 256), 256)
        sums = jnp.zeros((16, 256), jnp.float32)
        for z in range(4):
            sums = sums + jnp.sum((f32(part[z, :, :, :, at]) * f32(tokens[z, :, :, :, at])).reshape(16, 16, 256), axis=0)
        gain_acc[:, at] = sums[:8]
        gain_acc[:, also] = sums[8:]
        return carry

    lax.fori_loop(0, HALF // 256, gain_tile, 0)
    gain_slots[0, place[2]] = jnp.sum(gain_acc[...], axis=0, keepdims=True) / f32(gain[...])

    def gain_copy(phase, by, owner):
        axis = 2 - phase
        return pltpu.make_async_remote_copy(
            src_ref=gain_slots.at[phase, owner], dst_ref=gain_slots.at[phase, owner],
            send_sem=gain_send.at[phase, by - 1], recv_sem=gain_recv.at[phase, by - 1],
            device_id=neighbour(axis, by), device_id_type=MESH,
        )

    def gain_start(phase):
        for by in (1, 2, 3):
            go(gain_copy(phase, by, place[2 - phase]))

    def gain_sum(phase):
        for by in (1, 2, 3):
            gain_copy(phase, by, moved(2 - phase, -by)).wait_recv()
        return (gain_slots[phase, 0] + gain_slots[phase, 1]) + (gain_slots[phase, 2] + gain_slots[phase, 3])

    gain_start(0)
    line_sum(1)
    line_step(3)
    lax.fori_loop(4, 10, weight_tile, 0)
    settle(early)
    gain_slots[1, place[1]] = gain_sum(0)
    gain_start(1)
    line_sum(2)
    for turn in range(4):
        for sub in SUBS:
            rs_forward(1, sub, far_first(sub)[turn])
    sent = len(started)
    lax.fori_loop(10, 14, weight_tile, 0)
    gain_slots[2, place[0]] = gain_sum(1)
    gain_start(2)
    line_sum(3)
    for turn in range(3):
        for sub in SUBS:
            unit_by = far_first(sub)[turn]
            rs_sum(1, sub, unit_by)
            go(last_copy(sub, unit_by % 4))
    for sub in SUBS:
        rs_sum(1, sub, 0)
    lax.fori_loop(14, 16, weight_tile, 0)
    settle(sent)
    gain_grad[...] = gain_sum(2)
    kept = f32(tokens[place[1], place[0], (place[2] % 2) * 2 + place[2] // 2, :, HALF:])
    own[:, :HALF] = kept[:8]
    own[:, HALF:] = kept[8:]
    for sub in SUBS:
        _, _, lo, size = SCATTER[sub]
        for by in (1, 2, 3):
            last_copy(sub, by).wait_recv()
        columns = (slice(None), pl.ds(lo, size))
        summed = f32(got1[(2, place[SCATTER[sub][0][0]], *columns)])
        for by in (1, 2, 3):
            summed = summed + f32(got2[(by - 1, *columns)])
        total[:, pl.ds(lo, size)] = summed[:8]
        total[:, pl.ds(HALF + lo, size)] = summed[8:]
    settle(len(started))


def finish(
    up_grad, down_grad, total, unit, inverse, own, gain_grad, gain,
    input_out, gain_out, up_out, down_out,
    input_rows, sem,
):
    PIECES = 4
    copies = [pltpu.make_async_copy(gain_grad, gain_out, sem.at[0])]
    for piece in range(PIECES):
        for which, (source, target) in enumerate(((up_grad, up_out), (down_grad, down_out))):
            size = source.shape[0] // PIECES
            at = pl.ds(piece * size, size)
            copies.append(pltpu.make_async_copy(source.at[at, :], target.at[at, :], sem.at[2 + 2 * piece + which]))
    for copy in copies:
        copy.start()

    scaled = total[...] * f32(gain[...])
    units = unit[...]
    inner_mean = jnp.mean(scaled, axis=-1, keepdims=True)
    proj_mean = jnp.mean(scaled * units, axis=-1, keepdims=True)
    change = inverse[:, 0:1] * (scaled - inner_mean - units * proj_mean)
    input_rows[...] = (own[...] + change).astype(jnp.bfloat16)
    copies.append(pltpu.make_async_copy(input_rows, input_out, sem.at[1]))
    copies[-1].start()
    for copy in copies:
        copy.wait()


def on_device(upstream, saved_input, norm_gain, up_weight, down_weight):
    bf16, f4 = jnp.bfloat16, jnp.float32
    vmem, hbm = pl.BlockSpec(memory_space=pltpu.VMEM), pl.BlockSpec(memory_space=pl.ANY)
    dma = pltpu.SemaphoreType.DMA
    held = pl.pallas_call(
        kernel,
        out_shape=[
            pltpu.VMEM((D, HID), f4),
            pltpu.VMEM((HID, D), f4),
            pltpu.VMEM((ROWS, D), f4),
            pltpu.VMEM((ROWS, D), f4),
            pltpu.VMEM((ROWS, 128), f4),
            pltpu.VMEM((ROWS, D), f4),
            pltpu.VMEM((1, D), f4),
        ],
        in_specs=[vmem, vmem, vmem, hbm, hbm],
        out_specs=[vmem] * 7,
        scratch_shapes=[
            pltpu.VMEM((4, 4, 4, 16, D), bf16),
            pltpu.VMEM((2, 4, 4, 2, 16, HID), bf16),
            pltpu.VMEM((D, HID), bf16),
            pltpu.VMEM((4, 4, 4, 16, HALF), bf16),
            pltpu.VMEM((3, 4, 4, 16, HALF), bf16),
            pltpu.VMEM((3, 4, 16, HALF), bf16),
            pltpu.VMEM((3, 16, HALF), bf16),
            pltpu.VMEM((4, 4, 4, 16, 2 * HID), f4),
            pltpu.VMEM((16, HALF), bf16),
            pltpu.VMEM((ROWS, D), f4),
            pltpu.VMEM((3, 4, 1, D), f4),
            dma((3,)), dma((2,)),
            dma((6, 9, 3)), dma((6, 9, 3)), dma((6, 9, 3)), dma((6, 9, 3)),
            dma((3, 3)), dma((3, 3)),
        ],
        compiler_params=pltpu.CompilerParams(
            collective_id=0, has_side_effects=True, vmem_limit_bytes=42 * 2**20
        ),
        name="section_backward",
    )(upstream[0], saved_input[0], norm_gain, up_weight[0], down_weight[0].reshape(4, 4, 16, D))
    held = [pltpu.with_memory_space_constraint(array, pltpu.VMEM) for array in held]
    input_grad, gain_grad, up_grad, down_grad = pl.pallas_call(
        finish,
        out_shape=[
            jax.ShapeDtypeStruct((ROWS, D), bf16),
            jax.ShapeDtypeStruct((1, D), f4),
            jax.ShapeDtypeStruct((D, HID), f4),
            jax.ShapeDtypeStruct((HID, D), f4),
        ],
        in_specs=[vmem] * 8,
        out_specs=[hbm] * 4,
        scratch_shapes=[
            pltpu.VMEM((ROWS, D), bf16),
            dma((10,)),
        ],
        compiler_params=pltpu.CompilerParams(vmem_limit_bytes=4 * 2**20),
        name="finish",
    )(*held, norm_gain)
    return (input_grad[None], up_grad[None], down_grad[None], gain_grad)


def solution(mesh):
    in_specs = (
        P("section", ("dp", "tensor"), None),
        P("section", ("dp", "tensor"), None),
        P("section", None),
        P("section", None, ("dp", "tensor")),
        P("section", ("dp", "tensor"), None),
    )
    out_specs = (
        P("section", ("dp", "tensor"), None),
        P("section", None, ("dp", "tensor")),
        P("section", ("dp", "tensor"), None),
        P("section", None),
    )
    return jax.shard_map(
        on_device, mesh=mesh, in_specs=in_specs, out_specs=out_specs, check_vma=False
    )
```
